512 devices in a mesh: dp: 64 (over z, y_lo, core), tensor: 8 (over x, y_hi).
Axes of the slice: x: 4, y: 4 (y_hi: 2, y_lo: 2; y = y_hi * 2 + y_lo), z: 16, core: 2. Of those that a mesh axis runs over, the one named last changes fastest.
Arguments:
- activations: bfloat16 [98304, 2048], P('dp', 'tensor'), may hold values from -6 to 6
- out_grads: bfloat16 [98304, 2048], P('dp', 'tensor'), may hold values from -0.001953125 to 0.001953125
- left_stat: float32 [2048, 2048], P('dp', 'tensor'), may hold values from -1 to 11, as said below
- right_stat: float32 [2048, 2048], P('dp', 'tensor'), may hold values from -1 to 11, as said below
Outputs:
- left_new: float32 [2048, 2048], P('dp', 'tensor')
- right_new: float32 [2048, 2048], P('dp', 'tensor')
- update: float32 [2048, 2048], P('dp', 'tensor')
The draws below stay inside these ranges and needn't reach their ends.
Inputs may be any that keep to these rules, and one draw needn't show every extreme that they name: `left_stat`: symmetric, with a positive diagonal. `right_stat`: symmetric, with a positive diagonal.
All inputs are finite; a program needn't handle non-finite values.
Results may differ from the reference program's by a relative error of at most 0.0012.
Values may be sent and summed in bfloat16 or wider, within the bound.
A program may use at most 64 MiB of HBM per device.

```python
import math
import jax
import jax.numpy as jnp
from jax import lax

B = 2048
TOKENS = 98304


def stat_matrix(key):
    first_key, second_key = jax.random.split(key)
    noise = jax.random.normal(first_key, (B, B), jnp.float32)
    symmetric = (noise + noise.T) * (0.3 / math.sqrt(2 * B))
    diagonal = jnp.exp(jax.random.uniform(second_key, (B,), jnp.float32, math.log(0.25), math.log(4.0)))
    return symmetric + jnp.diag(diagonal)


def draw_left_stat(key, part):
    return stat_matrix(jax.random.fold_in(key, 11))


def draw_right_stat(key, part):
    return stat_matrix(jax.random.fold_in(key, 23))


def steps_of(own_key, dims, shards, least, largest):
    factor_of, own = 1.0, jax.random.fold_in(own_key, 6)
    for dim, blocks in shards:
        heights = jnp.exp(jax.random.uniform(jax.random.fold_in(own, dim), (blocks,), jnp.float32, least / len(shards), largest / len(shards)))
        factor_of = factor_of * jnp.repeat(heights, dims[dim] // blocks).reshape([-1 if axis == dim else 1 for axis in range(len(dims))])
    return factor_of


def scatter_about(stream_key, extent, deviation, most, cuts=(), dtype=jnp.bfloat16):
    drawn = deviation * jax.random.normal(stream_key, extent, jnp.float32)
    if cuts:
        drawn = drawn * steps_of(stream_key, extent, cuts, -0.22, 0.18)
    return jnp.clip(drawn, -most, most).astype(dtype)


def setup_inputs(seed: int = 0) -> dict:
    streams_of = jax.random.split(jax.random.key(seed), 5)
    activations = scatter_about(streams_of[0], (TOKENS, B), 1.0, 6.0, ((0, 64), (1, 8)))
    out_grads = scatter_about(streams_of[1], (TOKENS, B), (2 * (TOKENS * B) ** -0.5), 0.001953125, ((0, 64), (1, 8)))
    left_stat = draw_left_stat(jax.random.fold_in(streams_of[4], 71), 0)
    right_stat = draw_right_stat(jax.random.fold_in(streams_of[4], 71), 0)
    return dict(activations=activations, out_grads=out_grads, left_stat=left_stat, right_stat=right_stat)


def reference(activations, out_grads, left_stat, right_stat):
    highest = lax.Precision.HIGHEST
    gradient = lax.dot_general(activations, out_grads, (((0,), (0,)), ((), ())), preferred_element_type=jnp.float32)
    left_new = 0.9 * left_stat + 0.1 * jnp.dot(gradient, gradient.T, precision=highest, preferred_element_type=jnp.float32)
    right_new = 0.9 * right_stat + 0.1 * jnp.dot(gradient.T, gradient, precision=highest, preferred_element_type=jnp.float32)
    left_scale = jnp.sqrt(jnp.sum(left_new * left_new) / B + 1e-06)
    right_scale = jnp.sqrt(jnp.sum(right_new * right_new) / B + 1e-06)
    pre_left = 5.0 * gradient - jnp.dot(left_new, gradient, precision=highest, preferred_element_type=jnp.float32) / left_scale
    pre = 5.0 * pre_left - jnp.dot(pre_left, right_new, precision=highest, preferred_element_type=jnp.float32) / right_scale
    factor = jnp.sqrt(jnp.sum(gradient * gradient) + 1e-06) / jnp.sqrt(jnp.sum(pre * pre) + 1e-06)
    return (left_new, right_new, pre * factor)
```

```python
import jax
import jax.numpy as jnp
from jax import lax
from jax.experimental import pallas as pl
from jax.experimental.pallas import tpu as pltpu
from jax.sharding import Mesh
from jax.sharding import PartitionSpec as P

DP = ("z", "yl", "c")
TENSOR = ("x", "yh")
MESH = pl.DeviceIdType.MESH
F32 = jnp.float32
NEAR = (1, 15, 2)
BLOCKS = (0, 3, 1, 2)
TOKENS = 1536
HALF = 768
B = 2048


def dot(a, b, dims):
    return lax.dot_general(
        a, b, (dims, ((), ())), precision=lax.Precision.HIGHEST, preferred_element_type=F32
    )


def by_rows(a, b):
    return dot(a, b, ((1,), (1,)))


def by_columns(a, b):
    return dot(a.T, b, ((1,), (0,)))


def total(v):
    return jnp.sum(jnp.sum(v * v, axis=1, keepdims=True), axis=0, keepdims=True)


def kernel(
    a_ref, o_ref, ls_ref, rs_ref, left_ref, right_ref, update_ref,
    a_in, o_in, part, c_in, c_sum, y_in, tile, z1_in, z1_sum, z2_in, piece, grad, gz, stat,
    ls_in, hl, st, st_in, st_sum, qg, qg_in, ur, ur_in, la, turned, ub, uz, su, su_in, qu, qu_in,
    pr, pr_in, q_sum, qa, s_own, s1_in, s1_sum, s2_in,
    a_send, a_recv, send, recv, c_send, c_recv, y_send, y_recv, z_send, z_recv, ga_recv,
):
    z, yl, c = lax.axis_index("z"), lax.axis_index("yl"), lax.axis_index("c")
    x, yh = lax.axis_index("x"), lax.axis_index("yh")
    zh, zb, z1 = z // 4, z % 2, (z // 2) % 2
    ylc = 2 * yl + c
    place = ylc * 8 + x * 2 + yh

    def at(**other):
        return {**dict(z=z, yl=yl, c=c, x=x, yh=yh), **other}

    def x_peer(k):
        return at(x=lax.rem(x + k, 4))

    def z_peer(k):
        return at(z=lax.rem(z + k, 16))

    def flip(n, bit):
        return n + bit - 2 * n * bit

    def y_peer(d, **other):
        return at(c=flip(c, d % 2), yl=flip(yl, d // 2 % 2), yh=flip(yh, d // 4), **other)

    def plane_peer(d):
        bits = [flip((place >> i) % 2, (d >> i) % 2) for i in range(5)]
        return at(yh=bits[0], x=bits[1] + 2 * bits[2], c=bits[3], yl=bits[4])

    def remote(src, dst, s, r, peer):
        return pltpu.make_async_remote_copy(
            src_ref=src, dst_ref=dst, send_sem=s, recv_sem=r, device_id=peer, device_id_type=MESH
        )

    def settle(view, sem):
        pltpu.make_async_copy(view, view, sem).wait()

    barrier = pltpu.get_barrier_semaphore()

    def greet(peer):
        pl.semaphore_signal(barrier, inc=1, device_id=peer, device_id_type=MESH)

    def greet_plane(d, _):
        greet(plane_peer(d))
        return _

    def greet_column(k, _):
        greet(z_peer(k))
        greet(at(z=lax.rem(z + k, 16), yh=1 - yh))
        return _

    lax.fori_loop(1, 32, greet_plane, 0)
    lax.fori_loop(1, 16, greet_column, 0)
    z_pair = z + 2 - 4 * z1
    for d in (1, 2, 3, 5, 6, 7):
        greet(y_peer(d, z=z_pair))
    pl.semaphore_wait(barrier, 31 + 30 + 6)

    remote(o_ref, o_in, send.at[0], recv.at[0], at(yh=1 - yh)).start()

    def rows(h):
        return pl.ds(h * HALF, HALF)

    for slot, k, h in ((0, 1, 0), (1, 3, 1), (0, 1, 1), (1, 3, 0)):
        remote(
            a_ref.at[rows(h)], a_in.at[slot, rows(h)], a_send, a_recv.at[slot, h], x_peer(k)
        ).start()

    stat_to = stat.at[zh, zb, :, pl.ds(pl.multiple_of(yh * 256, 256), 256)]

    def send_stat(k, _):
        remote(rs_ref, stat_to, send.at[1], recv.at[1], at(z=lax.rem(z + k, 16), yh=z1)).start()
        return _

    lax.fori_loop(1, 16, send_stat, 0)
    own_stat = remote(rs_ref, stat_to, send.at[2], recv.at[1], at(yh=z1))
    pl.when(z1 == yh)(lambda: pltpu.make_async_copy(rs_ref, stat_to, recv.at[1]).start())
    pl.when(z1 != yh)(lambda: own_stat.start())
    ls_sends = []
    for b in range(2):
        zt = 4 * x + 2 * yh + b
        ls_from, ls_to = ls_ref.at[:, pl.ds(b * 128, 128)], ls_in.at[zh, zb]
        go = remote(ls_from, ls_to, send.at[3 + b], recv.at[2], at(z=zt, yh=z1))
        ls_sends.append((zt, go))

        def keep(ls_from=ls_from, ls_to=ls_to):
            pltpu.make_async_copy(ls_from, ls_to, recv.at[2]).start()

        pl.when(zt == z)(keep)
        pl.when(zt != z)(go.start)

    own_cols = pl.ds(pl.multiple_of(yh * 256, 256), 256)
    other_cols = pl.ds(pl.multiple_of((1 - yh) * 256, 256), 256)

    def terms(k, own):
        acts = a_ref[...] if k == 0 else a_in[k - 1]
        block = lax.dot_general(
            acts,
            o_ref[...] if own else o_in[...],
            (((0,), (0,)), ((), ())),
            preferred_element_type=F32,
        )
        part[k, :, :, :, :, own_cols if own else other_cols] = block.reshape(2, 2, 2, 32, 256)

    def block_of(k):
        return lax.rem(x + BLOCKS[k], 4)

    def c_start(k):
        remote(part.at[k, :, :, 1 - c], c_in.at[k], c_send.at[k], c_recv.at[k], at(c=1 - c)).start()

    def c_end(k):
        settle(c_in.at[k], c_recv.at[k])
        c_sum[k] = part[k, :, :, c] + c_in[k]
        remote(c_sum.at[k, :, 1 - yl], y_in.at[k], y_send.at[k], y_recv.at[k], at(yl=1 - yl)).start()

    def half_of(zz):
        return pl.ds(pl.multiple_of(flip((zz // 2) % 2, yh) * 16, 16), 16)

    def y_end(k):
        settle(y_in.at[k], y_recv.at[k])
        tile[k] = c_sum[k, :, yl] + y_in[k]
        for i, step in enumerate(NEAR):
            m = lax.rem(z + step, 16)
            remote(
                tile.at[k, m % 2, half_of(m)], z1_in.at[k, i], z_send.at[k], z_recv.at[k], z_peer(step)
            ).start()

    def z1_end(k):
        settle(z1_in.at[k], z_recv.at[k])
        z1_sum[k] = tile[k, zb, half_of(z)] + z1_in[k, 0] + z1_in[k, 1] + z1_in[k, 2]
        xb = block_of(k)
        far = lax.rem(xb - zh + 4, 4)

        def away():
            remote(
                z1_sum.at[k], z2_in.at[far - 1], send.at[5], recv.at[3], at(z=4 * xb + z % 4)
            ).start()

        def stay():
            piece[...] = z1_sum[k]

        pl.when(far != 0)(away)
        pl.when(far == 0)(stay)

    terms(0, True)
    settle(a_in.at[0, rows(0)], a_recv.at[0, 0])
    remote(a_in.at[0, rows(0)], a_in.at[2, rows(0)], a_send, a_recv.at[2, 0], x_peer(1)).start()
    settle(a_in.at[1, rows(1)], a_recv.at[1, 1])
    remote(a_in.at[1, rows(1)], a_in.at[2, rows(1)], a_send, a_recv.at[2, 1], x_peer(3)).start()
    settle(o_in, recv.at[0])
    terms(0, False)
    c_start(0)
    settle(a_in.at[0, rows(1)], a_recv.at[0, 1])
    terms(1, True)
    terms(1, False)
    c_start(1)
    c_end(0)
    settle(a_in.at[1, rows(0)], a_recv.at[1, 0])
    terms(2, True)
    terms(2, False)
    c_start(2)
    c_end(1)
    y_end(0)

    @pl.when(x == zh)
    def _():
        settle(ls_in, recv.at[2])
        for k in range(1, 4):
            remote(ls_in, hl.at[1], send.at[6], recv.at[4], x_peer(k)).start()
        pltpu.make_async_copy(ls_in, hl.at[1], recv.at[4]).start()

    settle(a_in.at[2, rows(0)], a_recv.at[2, 0])
    settle(a_in.at[2, rows(1)], a_recv.at[2, 1])
    terms(3, True)
    terms(3, False)
    c_start(3)
    c_end(2)
    y_end(1)
    z1_end(0)
    c_end(3)
    y_end(2)
    z1_end(1)
    y_end(3)
    z1_end(2)
    z1_end(3)
    settle(z2_in, recv.at[3])
    piece[...] = piece[...] + z2_in[0] + z2_in[1] + z2_in[2]

    mine = half_of(z)
    grad[zh, zb, mine] = piece[...]
    home = 4 * zh + 2 * yh + zb
    gz_rows = gz.at[pl.ds(pl.multiple_of(ylc * 32 + flip(z1, yh) * 16, 16), 16)]
    for i, step in enumerate((4, 12, 8)):
        remote(piece, grad.at[zh, zb, mine], send.at[7], ga_recv.at[i], z_peer(step)).start()
    for step in NEAR:
        remote(piece, grad.at[zh, zb, mine], send.at[8], recv.at[5], z_peer(step)).start()
    for d in range(1, 8):
        remote(piece, gz_rows, send.at[9], recv.at[6], y_peer(d, z=home)).start()
    gz_send = remote(piece, gz_rows, send.at[10], recv.at[6], at(z=home))
    pl.when(home == z)(lambda: pltpu.make_async_copy(piece, gz_rows, recv.at[6]).start())
    pl.when(home != z)(lambda: gz_send.start())
    for i, step in enumerate((4, 12, 8)):
        zs = lax.rem(zh + 4 - step // 4, 4)
        view = grad.at[zs, zb, mine]
        settle(view, ga_recv.at[i])
        for step2 in NEAR:
            remote(view, view, send.at[11], recv.at[5], z_peer(step2)).start()

    settle(gz, recv.at[6])
    settle(stat, recv.at[1])
    rows_z = gz[...]
    qg[...] = by_rows(stat[...].reshape(256, 512), rows_z).reshape(4, 64, 128)
    for k in range(1, 4):
        to = lax.rem(x + k, 4)
        remote(qg.at[to], qg_in.at[k - 1], send.at[12], recv.at[7], x_peer(k)).start()
    settle(grad.at[pl.ds(0, 3)], recv.at[5])

    @pl.when(x == zh)
    def _():
        cols = grad.at[:, :, :, pl.ds(pl.multiple_of(z % 4 * 128, 128), 128)]
        for k in range(1, 4):
            remote(cols, hl.at[0], send.at[13], recv.at[8], x_peer(k)).start()
        pltpu.make_async_copy(cols, hl.at[0], recv.at[8]).start()

    def tile_of():
        return grad[...].reshape(256, 512)

    st[...] = by_rows(tile_of(), rows_z)
    for k in range(1, 4):
        remote(st, st_in.at[k - 1], send.at[14], recv.at[9], x_peer(k)).start()
    settle(hl.at[0], recv.at[8])
    settle(hl.at[1], recv.at[4])
    ur[1] = by_columns(hl[0].reshape(256, 128), tile_of())
    settle(st_in, recv.at[9])
    st_sum[...] = st[...] + (st_in[0] + st_in[1] + st_in[2])
    lt = 0.9 * hl[1].reshape(256, 128) + 0.1 * st_sum[...]
    turned[...] = lt
    ur[0] = by_columns(lt, tile_of())

    def block_at(ref, d, *lead):
        r = pl.multiple_of((flip(c, d % 2) + 2 * flip(yl, d // 2 % 2)) * 32, 32)
        col = pl.multiple_of(flip(yh, d // 4) * 256, 256)
        return ref.at[(*lead, pl.ds(r, 32), pl.ds(col, 256))]

    for d in range(1, 8):
        remote(
            block_at(ur, d, slice(None)), ur_in.at[d - 1], send.at[15], recv.at[10], y_peer(d)
        ).start()
    own = turned[pl.ds(pl.multiple_of(x * 64, 64), 64), :]
    la[ylc] = own
    for d in range(1, 4):
        remote(la.at[ylc], la.at[ylc], send.at[16], recv.at[11], y_peer(d)).start()
    left_sq = total(own)
    grad_sq = total(piece[...])

    settle(ur_in, recv.at[10])
    u_block = block_at(ur, 0, 0)[...]
    r_block = block_at(ur, 0, 1)[...]
    for d in range(7):
        u_block = u_block + ur_in[d, 0]
        r_block = r_block + ur_in[d, 1]
    ub[...] = u_block
    block_at(uz, 0)[...] = u_block
    for d in range(1, 8):
        remote(ub, block_at(uz, 0), send.at[17], recv.at[12], y_peer(d)).start()
    right = 0.9 * rs_ref[...] + 0.1 * r_block
    right_ref[...] = right
    right_sq = total(right)
    lane = lax.broadcasted_iota(jnp.int32, (8, 128), 1)

    def sum_in_plane(n, values):
        v = jnp.zeros((8, 128), F32)
        for i, value in enumerate(values):
            v = jnp.where(lane == i, value, v)
        s_own[n] = v

        def out(d, _):
            remote(s_own.at[n], s1_in.at[n, d - 1], send.at[18 + n], recv.at[13 + n], plane_peer(d)).start()
            return _

        lax.fori_loop(1, 32, out, 0)

    def sum_along_z(n):
        settle(s1_in.at[n], recv.at[13 + n])
        s1_sum[n] = s_own[n] + jnp.sum(s1_in[n], axis=0)

        def out(k, _):
            remote(s1_sum.at[n], s2_in.at[n, k - 1], send.at[20 + n], recv.at[15 + n], z_peer(k)).start()
            return _

        lax.fori_loop(1, 16, out, 0)

    def sums(n, count):
        settle(s2_in.at[n], recv.at[15 + n])
        v = s1_sum[n] + jnp.sum(s2_in[n], axis=0)
        first = lax.broadcasted_iota(jnp.int32, (8, 128), 0) == 0
        picked = [jnp.where((lane == i) & first, v, 0.0) for i in range(count)]
        return [jnp.sum(jnp.sum(p, axis=1, keepdims=True), axis=0, keepdims=True) for p in picked]

    sum_in_plane(0, (left_sq, right_sq, grad_sq))

    settle(uz.at[pl.ds(0, 112)], recv.at[12])
    rows_u = uz[...]
    su[...] = by_rows(tile_of(), rows_u)
    for k in range(1, 4):
        remote(su, su_in.at[k - 1], send.at[22], recv.at[17], x_peer(k)).start()
    qu[...] = by_rows(stat[...].reshape(256, 512), rows_u).reshape(4, 64, 128)
    for k in range(1, 4):
        to = lax.rem(x + k, 4)
        remote(qu.at[to], qu_in.at[k - 1], send.at[23], recv.at[18], x_peer(k)).start()
    sum_along_z(0)

    def assembled(slots):
        v = slots[...].reshape(4, 2, 32, 128)
        whole = jnp.concatenate([v[i, b] for b in range(2) for i in range(4)], axis=0)
        return whole.T

    settle(la.at[pl.ds(0, 3)], recv.at[11])
    lt_rows = assembled(la)
    uz_rows = pl.ds(pl.multiple_of(ylc * 32, 32), 32)
    pr[:, 0:256] = lt_rows
    left_ref[...] = pr[uz_rows, 0:256]

    settle(su_in, recv.at[17])
    s_u = su[...] + (su_in[0] + su_in[1] + su_in[2])
    settle(qg_in, recv.at[7])
    settle(qu_in, recv.at[18])
    left_total, right_total, grad_total = sums(0, 3)
    left_scale = jnp.sqrt(left_total / B + 1e-06)
    right_scale = jnp.sqrt(right_total / B + 1e-06)
    q_g = qg[x] + qg_in[0] + qg_in[1] + qg_in[2]
    q_u = qu[x] + qu_in[0] + qu_in[1] + qu_in[2]
    q_sum[...] = 0.9 * (5.0 * q_g - q_u / left_scale)
    qa[ylc] = q_sum[...]
    for d in range(1, 4):
        remote(q_sum, qa.at[ylc], send.at[24], recv.at[19], y_peer(d)).start()
    pr[...] = by_columns(0.1 * (5.0 * st_sum[...] - s_u / left_scale), tile_of())
    for d in range(1, 8):
        remote(block_at(pr, d), pr_in.at[d - 1], send.at[25], recv.at[20], y_peer(d)).start()
    pre_left = 5.0 * block_at(gz, 0)[...] - ub[...] / left_scale
    settle(qa.at[pl.ds(0, 3)], recv.at[19])
    turned[pl.ds(0, 128), :] = assembled(qa)[:, 0:128]
    turned[pl.ds(128, 128), :] = assembled(qa)[:, 128:256]
    low = turned[pl.ds(pl.multiple_of(ylc * 32, 32), 32), :]
    high = turned[pl.ds(pl.multiple_of(128 + ylc * 32, 32), 32), :]
    product = jnp.concatenate([low, high], axis=1) + block_at(pr, 0)[...]
    settle(pr_in, recv.at[20])
    for d in range(7):
        product = product + pr_in[d]
    pre = 5.0 * pre_left - product / right_scale
    sum_in_plane(1, (total(pre),))
    sum_along_z(1)
    (pre_total,) = sums(1, 1)
    update_ref[...] = pre * (jnp.sqrt(grad_total + 1e-06) / jnp.sqrt(pre_total + 1e-06))

    settle(o_in, send.at[0])
    settle(a_in, a_send)
    settle(ur.at[:, pl.ds(0, 120)], send.at[1])
    pl.when(z1 != yh)(own_stat.wait_send)
    for zt, go in ls_sends:
        pl.when(zt != z)(go.wait_send)
    for k in range(4):
        settle(c_in.at[k], c_send.at[k])
        settle(y_in.at[k], y_send.at[k])
        settle(z1_in.at[k], z_send.at[k])
    settle(z2_in, send.at[5])
    settle(z2_in, send.at[7])
    settle(z2_in, send.at[8])
    settle(gz.at[pl.ds(0, 112)], send.at[9])
    pl.when(home != z)(gz_send.wait_send)
    settle(grad.at[pl.ds(0, 3), :, pl.ds(0, 24)], send.at[11])
    settle(qg_in, send.at[12])

    @pl.when(x == zh)
    def _():
        settle(st_in, send.at[6])
        settle(st_in, send.at[13])

    settle(st_in, send.at[14])
    settle(ur_in, send.at[15])
    settle(qg_in, send.at[16])
    settle(pr_in, send.at[17])
    for n in range(2):
        settle(s1_in.at[n], send.at[18 + n])
        settle(s2_in.at[n], send.at[20 + n])
    settle(st_in, send.at[22])
    settle(qg_in, send.at[23])
    settle(qg_in, send.at[24])
    settle(pr_in, send.at[25])


def local(activations, out_grads, left_stat, right_stat):
    vmem = pl.BlockSpec(memory_space=pltpu.VMEM)
    block = jax.ShapeDtypeStruct((32, 256), F32)
    bf16 = jnp.bfloat16
    shapes = [
        ((3, TOKENS, 256), bf16), ((TOKENS, 256), bf16),
        ((4, 2, 2, 2, 32, 512), F32), ((4, 2, 2, 32, 512), F32),
        ((4, 2, 2, 32, 512), F32), ((4, 2, 32, 512), F32),
        ((4, 2, 32, 512), F32), ((4, 3, 16, 512), F32),
        ((4, 16, 512), F32), ((3, 16, 512), F32), ((16, 512), F32),
        ((4, 2, 32, 512), F32), ((128, 512), F32), ((4, 2, 32, 512), F32),
        ((4, 2, 32, 128), F32), ((2, 4, 2, 32, 128), F32),
        ((256, 128), F32), ((3, 256, 128), F32), ((256, 128), F32),
        ((4, 64, 128), F32), ((3, 64, 128), F32),
        ((2, 128, 512), F32), ((7, 2, 32, 256), F32),
        ((4, 64, 128), F32), ((256, 128), F32), ((32, 256), F32), ((128, 512), F32),
        ((256, 128), F32), ((3, 256, 128), F32),
        ((4, 64, 128), F32), ((3, 64, 128), F32),
        ((128, 512), F32), ((7, 32, 256), F32),
        ((64, 128), F32), ((4, 64, 128), F32),
        ((2, 8, 128), F32), ((2, 31, 8, 128), F32),
        ((2, 8, 128), F32), ((2, 15, 8, 128), F32),
    ]
    dma = pltpu.SemaphoreType.DMA
    sems = [dma, dma((3, 2)), dma((26,)), dma((21,))] + [dma((4,))] * 6 + [dma((3,))]
    return pl.pallas_call(
        kernel,
        out_shape=(block, block, block),
        in_specs=[vmem] * 4,
        out_specs=(vmem, vmem, vmem),
        scratch_shapes=[pltpu.VMEM(s, d) for s, d in shapes] + sems,
        compiler_params=pltpu.CompilerParams(
            collective_id=0, has_side_effects=True, vmem_limit_bytes=58 * 2**20
        ),
        cost_estimate=pl.CostEstimate(flops=2 * 10**9, bytes_accessed=4 * 10**6, transcendentals=0),
    )(activations, out_grads, left_stat, right_stat)


def solution(mesh):
    finer = Mesh(mesh.devices.reshape(16, 2, 2, 4, 2), ("z", "yl", "c", "x", "yh"))
    spec = P(DP, TENSOR)
    return jax.shard_map(
        local,
        mesh=finer,
        in_specs=(spec,) * 4,
        out_specs=(spec,) * 3,
        check_vma=False,
    )
```

```python
import jax
import jax.numpy as jnp
from jax import lax
from jax.experimental import pallas as pl
from jax.experimental.pallas import tpu as pltpu
from jax.sharding import Mesh
from jax.sharding import PartitionSpec as P

DP = ("z", "yl", "c")
TENSOR = ("x", "yh")
MESH = pl.DeviceIdType.MESH
F32 = jnp.float32
NEAR = (1, 15, 2)
FAR = (4, 12, 8)
DIRECT = (3,)
BLOCKS = (0, 3, 1, 2)
TOKENS = 1536
HALF = 768
B = 2048


def dot(a, b, dims):
    return lax.dot_general(a, b, (dims, ((), ())), preferred_element_type=F32)


def parts(v):
    high = v.astype(jnp.bfloat16)
    return high, (v - high.astype(F32)).astype(jnp.bfloat16)


def by_rows(a, b):
    high, low = parts(b)
    over = ((1,), (1,))
    small = dot(a[0], low, over)
    if len(a) == 2:
        small = small + dot(a[1], high, over)
    return dot(a[0], high, over) + small


def by_columns(a, b):
    high, low = parts(a.T)
    over = ((1,), (0,))
    return dot(high, b[0], over) + (dot(low, b[0], over) + dot(high, b[1], over))


def total(v):
    return jnp.sum(jnp.sum(v * v, axis=1, keepdims=True), axis=0, keepdims=True)


def kernel(
    a_ref, o_ref, ls_ref, rs_ref, left_ref, right_ref, update_ref,
    a_own, o_own, a_in, o_in, part, c_in, c_sum, y_in, tile, z1_in, z1_sum, z2_in, grad, g_parts, gz, stat, rs_half,
    ls_in, hl, st, st_in, st_sum, qg, qg_in, ur, ur_in, la, turned, ub, uz, su, su_in, qu, qu_in,
    pr, pr_in, q_sum, qa, s_own, s1_in, s1_sum, s2_in,
    a_send, a_recv, send, recv, c_send, c_recv, y_send, y_recv, z_send, z_recv, z2_send, z2_recv,
    far_send, far_recv, near_send, near_recv, s_sems, relay,
):
    z, yl, c = lax.axis_index("z"), lax.axis_index("yl"), lax.axis_index("c")
    x, yh = lax.axis_index("x"), lax.axis_index("yh")
    zh, zb, z1 = z // 4, z % 2, (z // 2) % 2
    ylc = 2 * yl + c
    place = ylc * 8 + x * 2 + yh

    def at(**other):
        return {**dict(z=z, yl=yl, c=c, x=x, yh=yh), **other}

    def x_peer(k):
        return at(x=lax.rem(x + k, 4))

    def z_peer(k):
        return at(z=lax.rem(z + k, 16))

    def flip(n, bit):
        return n + bit - 2 * n * bit

    def y_peer(d, **other):
        return at(c=flip(c, d % 2), yl=flip(yl, d // 2 % 2), yh=flip(yh, d // 4), **other)

    bits = [(yh, 1 - yh), None, None, (c, 1 - c), (yl, 1 - yl)]
    xs = [flip(x % 2, k % 2) + 2 * flip(x // 2, k // 2) for k in range(4)]

    def plane_peer(d):
        return at(yh=bits[0][d % 2], x=xs[d // 2 % 4], c=bits[3][d // 8 % 2], yl=bits[4][d // 16])

    def remote(src, dst, s, r, peer):
        return pltpu.make_async_remote_copy(
            src_ref=src, dst_ref=dst, send_sem=s, recv_sem=r, device_id=peer, device_id_type=MESH
        )

    def settle(view, sem):
        pltpu.make_async_copy(view, view, sem).wait()

    drain = []

    def sent(view, sem):
        drain.append(lambda: settle(view, sem))

    barrier = pltpu.get_barrier_semaphore()

    def greet(peer):
        pl.semaphore_signal(barrier, inc=1, device_id=peer, device_id_type=MESH)

    copies = [
        pltpu.make_async_copy(a_ref, a_own, send.at[7]),
        pltpu.make_async_copy(o_ref, o_own, send.at[8]),
    ]
    for copy in copies:
        copy.start()
    for d in range(1, 32):
        greet(plane_peer(d))
    for k in (1, 2, 14, 15):
        greet(z_peer(k))
    pl.semaphore_wait(barrier, 31 + 4)

    def tell(n, k):
        pl.semaphore_signal(relay.at[n], inc=1, device_id=z_peer(k), device_id_type=MESH)

    remote(o_ref, o_in, send.at[11], recv.at[0], at(yh=1 - yh)).start()
    sent(o_in, send.at[11])
    sent(a_in, a_send)

    def rows(h):
        return pl.ds(h * HALF, HALF)

    for slot, k, h in ((0, 1, 0), (1, 3, 1), (0, 1, 1), (1, 3, 0)):
        remote(
            a_ref.at[rows(h)], a_in.at[slot, rows(h)], a_send, a_recv.at[slot, h], x_peer(k)
        ).start()

    for k in (1, 2, 14, 15):
        tell(0, k)

    own_cols = pl.ds(pl.multiple_of(yh * 256, 256), 256)
    other_cols = pl.ds(pl.multiple_of((1 - yh) * 256, 256), 256)

    def terms(k, own):
        acts = a_own[...] if k == 0 else a_in[k - 1]
        block = lax.dot_general(
            acts,
            o_own[...] if own else o_in[...],
            (((0,), (0,)), ((), ())),
            preferred_element_type=F32,
        )
        part[k, :, :, :, :, own_cols if own else other_cols] = block.reshape(2, 2, 2, 32, 256)

    def block_of(k):
        return lax.rem(x + BLOCKS[k], 4)

    def c_start(k):
        remote(part.at[k, :, :, 1 - c], c_in.at[k], c_send.at[k], c_recv.at[k], at(c=1 - c)).start()
        sent(c_in.at[k], c_send.at[k])

    def c_end(k):
        settle(c_in.at[k], c_recv.at[k])
        c_sum[k] = part[k, :, :, c] + c_in[k]
        remote(c_sum.at[k, :, 1 - yl], y_in.at[k], y_send.at[k], y_recv.at[k], at(yl=1 - yl)).start()
        sent(y_in.at[k], y_send.at[k])

    def half_of(zz):
        return pl.ds(pl.multiple_of(flip((zz // 2) % 2, yh) * 16, 16), 16)

    def y_end(k):
        settle(y_in.at[k], y_recv.at[k])
        tile[k] = c_sum[k, :, yl] + y_in[k]
        for i, step in enumerate(NEAR):
            m = lax.rem(z + step, 16)
            remote(
                tile.at[k, m % 2, half_of(m)], z1_in.at[k, i], z_send.at[k], z_recv.at[k], z_peer(step)
            ).start()
        sent(z1_in.at[k], z_send.at[k])

    mine = half_of(z)

    def columns_of(zz):
        return pl.ds(pl.multiple_of(zz * 128, 128), 128)

    def z1_end(k):
        settle(z1_in.at[k], z_recv.at[k])
        z1_sum[k] = tile[k, zb, mine] + z1_in[k, 0] + z1_in[k, 1] + z1_in[k, 2]
        if k in DIRECT:
            for i, step in enumerate(FAR):
                remote(z1_sum.at[k], z2_in.at[k, i], z2_send.at[k], z2_recv.at[k], z_peer(step)).start()
            sent(z2_in.at[k], z2_send.at[k])
            return
        for i, step in enumerate(FAR):
            at_zh = columns_of(lax.rem(zh + step // 4, 4))
            remote(
                z1_sum.at[k, :, at_zh], z2_in.at[k, i, :, at_zh], z2_send.at[k], z2_recv.at[k], z_peer(step)
            ).start()
        sent(z2_in.at[k, :, :, pl.ds(0, 128)], z2_send.at[k])

    def piece_of(k):
        return grad.at[block_of(k), zb, mine]

    def z2_own(k):
        if k in DIRECT:
            return
        settle(z2_in.at[k, :, :, pl.ds(0, 128)], z2_recv.at[k])
        cols = columns_of(zh)
        mine_k = grad.at[block_of(k), zb, mine, cols]
        mine_k[...] = z1_sum[k, :, cols] + (z2_in[k, 0, :, cols] + z2_in[k, 1, :, cols] + z2_in[k, 2, :, cols])
        for step in FAR:
            remote(mine_k, mine_k, far_send.at[k], far_recv.at[k], z_peer(step)).start()
        sent(z2_in.at[k, :, :, pl.ds(0, 128)], far_send.at[k])

    def z2_end(k):
        if k in DIRECT:
            settle(z2_in.at[k], z2_recv.at[k])
            piece_of(k)[...] = z1_sum[k] + (z2_in[k, 0] + z2_in[k, 1] + z2_in[k, 2])
        else:
            settle(z2_in.at[k, :, :, pl.ds(0, 128)], far_recv.at[k])
        for step in NEAR:
            remote(piece_of(k), piece_of(k), near_send.at[k], near_recv.at[k], z_peer(step)).start()
        sent(z2_in.at[k], near_send.at[k])

    def z3_end(k):
        settle(z2_in.at[k], near_recv.at[k])
        xb = block_of(k)
        high, low = parts(grad[xb].reshape(64, 512))
        g_parts[0, xb] = high
        g_parts[1, xb] = low

    rs_half[...] = rs_ref[...].astype(jnp.bfloat16)
    for copy in copies:
        copy.wait()
    terms(0, True)
    pl.semaphore_wait(relay.at[0], 4)
    for k in (3, 4, 12, 13):
        tell(1, k)
    settle(a_in.at[0, rows(0)], a_recv.at[0, 0])
    remote(a_in.at[0, rows(0)], a_in.at[2, rows(0)], a_send, a_recv.at[2, 0], x_peer(1)).start()
    settle(a_in.at[1, rows(1)], a_recv.at[1, 1])
    remote(a_in.at[1, rows(1)], a_in.at[2, rows(1)], a_send, a_recv.at[2, 1], x_peer(3)).start()
    pl.semaphore_wait(relay.at[1], 4)
    tell(2, 4)
    tell(2, 12)

    pl.semaphore_wait(relay.at[2], 2)

    stat_to = stat.at[zh, zb, :, pl.ds(pl.multiple_of(yh * 256, 256), 256)]
    for step in FAR:
        remote(rs_half, stat_to, send.at[1], recv.at[1], at(z=lax.rem(z + step, 16), yh=z1)).start()
    own_stat = remote(rs_half, stat_to, send.at[2], recv.at[1], at(yh=z1))
    pl.when(z1 == yh)(lambda: pltpu.make_async_copy(rs_half, stat_to, recv.at[1]).start())
    pl.when(z1 != yh)(lambda: own_stat.start())
    sent(stat.at[pl.ds(0, 3), 0, :, pl.ds(0, 256)], send.at[1])
    drain.append(lambda: pl.when(z1 != yh)(own_stat.wait_send))
    for b in range(2):
        zt = 4 * x + 2 * yh + b
        ls_from, ls_to = ls_ref.at[:, pl.ds(b * 128, 128)], ls_in.at[zh, zb]
        go = remote(ls_from, ls_to, send.at[3 + b], recv.at[2], at(z=zt, yh=z1))
        drain.append(lambda zt=zt, go=go: pl.when(zt != z)(go.wait_send))

        def keep(ls_from=ls_from, ls_to=ls_to):
            pltpu.make_async_copy(ls_from, ls_to, recv.at[2]).start()

        pl.when(zt == z)(keep)
        pl.when(zt != z)(go.start)

    settle(o_in, recv.at[0])
    terms(0, False)
    c_start(0)
    settle(a_in.at[0, rows(1)], a_recv.at[0, 1])
    terms(1, True)
    terms(1, False)
    c_start(1)

    @pl.when(z1 == yh)
    def _():
        view = stat.at[:, zb]
        settle(view, recv.at[1])
        for step in NEAR:
            remote(view, view, send.at[5], recv.at[3], z_peer(step)).start()

    drain.append(lambda: pl.when(z1 == yh)(lambda: settle(z2_in, send.at[5])))

    c_end(0)
    settle(a_in.at[1, rows(0)], a_recv.at[1, 0])
    terms(2, True)
    terms(2, False)
    c_start(2)
    c_end(1)
    c_end(2)
    y_end(0)

    settle(a_in.at[2, rows(0)], a_recv.at[2, 0])
    settle(a_in.at[2, rows(1)], a_recv.at[2, 1])
    terms(3, True)
    terms(3, False)
    c_start(3)

    @pl.when(x == zh)
    def _():
        settle(ls_in, recv.at[2])
        for k in range(1, 4):
            remote(ls_in, hl.at[1], send.at[6], recv.at[4], x_peer(k)).start()
        pltpu.make_async_copy(ls_in, hl.at[1], recv.at[4]).start()

    drain.append(lambda: pl.when(x == zh)(lambda: settle(st_in, send.at[6])))

    y_end(1)
    z1_end(0)
    c_end(3)
    y_end(2)
    z1_end(1)
    y_end(3)
    z1_end(2)
    z2_own(0)
    z1_end(3)
    z2_own(1)
    z2_own(2)
    z2_end(0)
    z2_end(1)
    z2_own(3)
    z2_end(2)
    z3_end(0)
    z2_end(3)

    home = 4 * zh + 2 * yh + zb
    gz_rows = gz.at[pl.ds(pl.multiple_of(ylc * 32 + flip(z1, yh) * 16, 16), 16)]
    piece = grad.at[zh, zb, mine]
    for d in range(1, 8):
        remote(piece, gz_rows, send.at[9], recv.at[6], y_peer(d, z=home)).start()
    gz_send = remote(piece, gz_rows, send.at[10], recv.at[6], at(z=home))
    pl.when(home == z)(lambda: pltpu.make_async_copy(piece, gz_rows, recv.at[6]).start())
    pl.when(home != z)(lambda: gz_send.start())
    sent(gz.at[pl.ds(0, 112)], send.at[9])
    drain.append(lambda: pl.when(home != z)(gz_send.wait_send))
    z3_end(1)
    z3_end(2)
    z3_end(3)
    settle(gz, recv.at[6])
    rows_z = gz[...]

    def tile_of():
        return g_parts[0].reshape(256, 512), g_parts[1].reshape(256, 512)

    st[...] = by_rows(tile_of(), rows_z)
    for k in range(1, 4):
        remote(st, st_in.at[k - 1], send.at[14], recv.at[9], x_peer(k)).start()
    sent(st_in, send.at[14])

    @pl.when(x == zh)
    def _():
        cols = grad.at[:, :, :, pl.ds(pl.multiple_of(z % 4 * 128, 128), 128)]
        for k in range(1, 4):
            remote(cols, hl.at[0], send.at[13], recv.at[8], x_peer(k)).start()
        pltpu.make_async_copy(cols, hl.at[0], recv.at[8]).start()

    drain.append(lambda: pl.when(x == zh)(lambda: settle(st_in, send.at[13])))
    settle(hl.at[1], recv.at[4])
    settle(st_in, recv.at[9])
    st_sum[...] = st[...] + (st_in[0] + st_in[1] + st_in[2])
    lt = 0.9 * hl[1].reshape(256, 128) + 0.1 * st_sum[...]
    turned[...] = lt
    ur[0] = by_columns(lt, tile_of())

    def block_at(ref, d, *lead):
        r = pl.multiple_of((flip(c, d % 2) + 2 * flip(yl, d // 2 % 2)) * 32, 32)
        col = pl.multiple_of(flip(yh, d // 4) * 256, 256)
        return ref.at[(*lead, pl.ds(r, 32), pl.ds(col, 256))]

    for d in range(1, 8):
        remote(
            block_at(ur, d, 0), ur_in.at[0, d - 1], send.at[15], recv.at[10], y_peer(d)
        ).start()
    sent(ur_in.at[0], send.at[15])
    own = turned[pl.ds(pl.multiple_of(x * 64, 64), 64), :]
    la[ylc] = own
    for d in range(1, 4):
        remote(la.at[ylc], la.at[ylc], send.at[16], recv.at[11], y_peer(d)).start()
    sent(qg_in, send.at[16])
    lane = lax.broadcasted_iota(jnp.int32, (8, 128), 1)

    def sum_in_plane(n, values):
        v = jnp.zeros((8, 128), F32)
        for i, value in enumerate(values):
            v = jnp.where(lane == i, value, v)
        s_own[n] = v

        for d in range(1, 32):
            remote(s_own.at[n], s1_in.at[n, d - 1], s_sems.at[0, n], s_sems.at[1, n], plane_peer(d)).start()
        sent(s1_in.at[n], s_sems.at[0, n])

    def sum_along_z(n):
        settle(s1_in.at[n], s_sems.at[1, n])
        s1_sum[n] = s_own[n] + jnp.sum(s1_in[n], axis=0)

        for k in range(1, 16):
            remote(s1_sum.at[n], s2_in.at[n, k - 1], s_sems.at[2, n], s_sems.at[3, n], z_peer(k)).start()
        sent(s2_in.at[n], s_sems.at[2, n])

    def sums(n, count):
        settle(s2_in.at[n], s_sems.at[3, n])
        v = s1_sum[n] + jnp.sum(s2_in[n], axis=0)
        first = lax.broadcasted_iota(jnp.int32, (8, 128), 0) == 0
        picked = [jnp.where((lane == i) & first, v, 0.0) for i in range(count)]
        return [jnp.sum(jnp.sum(p, axis=1, keepdims=True), axis=0, keepdims=True) for p in picked]

    sum_in_plane(0, (total(own), total(piece[...])))
    settle(hl.at[0], recv.at[8])
    ur[1] = by_columns(hl[0].reshape(256, 128), tile_of())
    for d in range(1, 8):
        remote(
            block_at(ur, d, 1), ur_in.at[1, d - 1], send.at[0], recv.at[5], y_peer(d)
        ).start()
    drain.append(lambda: settle(ur_in.at[1], send.at[0]))

    settle(ur_in.at[0], recv.at[10])
    u_block = block_at(ur, 0, 0)[...]
    for d in range(7):
        u_block = u_block + ur_in[0, d]
    ub[...] = u_block
    block_at(uz, 0)[...] = u_block
    for d in range(1, 8):
        remote(ub, block_at(uz, 0), send.at[17], recv.at[12], y_peer(d)).start()
    sent(pr_in, send.at[17])
    sum_along_z(0)

    settle(uz.at[pl.ds(0, 112)], recv.at[12])
    rows_u = uz[...]
    su[...] = by_rows(tile_of(), rows_u)
    for k in range(1, 4):
        remote(su, su_in.at[k - 1], send.at[22], recv.at[17], x_peer(k)).start()
    sent(st_in, send.at[22])
    settle(ur_in.at[1], recv.at[5])
    r_block = block_at(ur, 0, 1)[...]
    for d in range(7):
        r_block = r_block + ur_in[1, d]
    right = 0.9 * rs_ref[...] + 0.1 * r_block
    right_ref[...] = right
    sum_in_plane(1, (total(right),))
    pl.when(z1 == yh)(lambda: settle(stat.at[:, 0], recv.at[3]))
    pl.when(z1 != yh)(lambda: settle(stat, recv.at[3]))
    qg[...] = by_rows((stat[...].reshape(256, 512),), rows_z).reshape(4, 64, 128)
    for k in range(1, 4):
        to = lax.rem(x + k, 4)
        remote(qg.at[to], qg_in.at[k - 1], send.at[12], recv.at[7], x_peer(k)).start()
    sent(qg_in, send.at[12])
    qu[...] = by_rows((stat[...].reshape(256, 512),), rows_u).reshape(4, 64, 128)
    for k in range(1, 4):
        to = lax.rem(x + k, 4)
        remote(qu.at[to], qu_in.at[k - 1], send.at[23], recv.at[18], x_peer(k)).start()
    sent(qg_in, send.at[23])
    sum_along_z(1)

    def assembled(slots):
        v = slots[...].reshape(4, 2, 32, 128)
        whole = jnp.concatenate([v[i, b] for b in range(2) for i in range(4)], axis=0)
        return whole.T

    settle(la.at[pl.ds(0, 3)], recv.at[11])
    lt_rows = assembled(la)
    uz_rows = pl.ds(pl.multiple_of(ylc * 32, 32), 32)
    pr[:, 0:256] = lt_rows
    left_ref[...] = pr[uz_rows, 0:256]

    settle(su_in, recv.at[17])
    s_u = su[...] + (su_in[0] + su_in[1] + su_in[2])
    settle(qg_in, recv.at[7])
    settle(qu_in, recv.at[18])
    left_total, grad_total = sums(0, 2)
    left_scale = jnp.sqrt(left_total / B + 1e-06)
    q_g = qg[x] + qg_in[0] + qg_in[1] + qg_in[2]
    q_u = qu[x] + qu_in[0] + qu_in[1] + qu_in[2]
    q_sum[...] = 0.9 * (5.0 * q_g - q_u / left_scale)
    qa[ylc] = q_sum[...]
    for d in range(1, 4):
        remote(q_sum, qa.at[ylc], send.at[24], recv.at[19], y_peer(d)).start()
    sent(qg_in, send.at[24])
    pr[...] = by_columns(0.1 * (5.0 * st_sum[...] - s_u / left_scale), tile_of())
    for d in range(1, 8):
        remote(block_at(pr, d), pr_in.at[d - 1], send.at[25], recv.at[20], y_peer(d)).start()
    sent(pr_in, send.at[25])
    pre_left = 5.0 * block_at(gz, 0)[...] - ub[...] / left_scale
    settle(qa.at[pl.ds(0, 3)], recv.at[19])
    turned[pl.ds(0, 128), :] = assembled(qa)[:, 0:128]
    turned[pl.ds(128, 128), :] = assembled(qa)[:, 128:256]
    low = turned[pl.ds(pl.multiple_of(ylc * 32, 32), 32), :]
    high = turned[pl.ds(pl.multiple_of(128 + ylc * 32, 32), 32), :]
    product = jnp.concatenate([low, high], axis=1) + block_at(pr, 0)[...]
    settle(pr_in, recv.at[20])
    for d in range(7):
        product = product + pr_in[d]
    (right_total,) = sums(1, 1)
    right_scale = jnp.sqrt(right_total / B + 1e-06)
    pre = 5.0 * pre_left - product / right_scale
    sum_in_plane(2, (total(pre),))
    sum_along_z(2)
    (pre_total,) = sums(2, 1)
    update_ref[...] = pre * (jnp.sqrt(grad_total + 1e-06) / jnp.sqrt(pre_total + 1e-06))

    for wait in drain:
        wait()


def local(activations, out_grads, left_stat, right_stat):
    vmem = pl.BlockSpec(memory_space=pltpu.VMEM)
    block = jax.ShapeDtypeStruct((32, 256), F32)
    bf16 = jnp.bfloat16
    shapes = [
        ((TOKENS, 256), bf16), ((TOKENS, 256), bf16),
        ((3, TOKENS, 256), bf16), ((TOKENS, 256), bf16),
        ((4, 2, 2, 2, 32, 512), F32), ((4, 2, 2, 32, 512), F32),
        ((4, 2, 2, 32, 512), F32), ((4, 2, 32, 512), F32),
        ((4, 2, 32, 512), F32), ((4, 3, 16, 512), F32),
        ((4, 16, 512), F32), ((4, 3, 16, 512), F32),
        ((4, 2, 32, 512), F32), ((2, 4, 64, 512), bf16), ((128, 512), F32),
        ((4, 2, 32, 512), bf16), ((32, 256), bf16),
        ((4, 2, 32, 128), F32), ((2, 4, 2, 32, 128), F32),
        ((256, 128), F32), ((3, 256, 128), F32), ((256, 128), F32),
        ((4, 64, 128), F32), ((3, 64, 128), F32),
        ((2, 128, 512), F32), ((2, 7, 32, 256), F32),
        ((4, 64, 128), F32), ((256, 128), F32), ((32, 256), F32), ((128, 512), F32),
        ((256, 128), F32), ((3, 256, 128), F32),
        ((4, 64, 128), F32), ((3, 64, 128), F32),
        ((128, 512), F32), ((7, 32, 256), F32),
        ((64, 128), F32), ((4, 64, 128), F32),
        ((3, 8, 128), F32), ((3, 31, 8, 128), F32),
        ((3, 8, 128), F32), ((3, 15, 8, 128), F32),
    ]
    dma = pltpu.SemaphoreType.DMA
    sems = [dma, dma((3, 2)), dma((26,)), dma((21,))] + [dma((4,))] * 12
    sems += [dma((4, 3)), pltpu.SemaphoreType.REGULAR((3,))]
    return pl.pallas_call(
        kernel,
        out_shape=(block, block, block),
        in_specs=[pl.BlockSpec(memory_space=pl.ANY)] * 2 + [vmem] * 2,
        out_specs=(vmem, vmem, vmem),
        scratch_shapes=[pltpu.VMEM(s, d) for s, d in shapes] + sems,
        compiler_params=pltpu.CompilerParams(
            collective_id=0, has_side_effects=True, vmem_limit_bytes=60 * 2**20
        ),
        cost_estimate=pl.CostEstimate(flops=2 * 10**9, bytes_accessed=4 * 10**6, transcendentals=0),
    )(activations, out_grads, left_stat, right_stat)


def solution(mesh):
    finer = Mesh(mesh.devices.reshape(16, 2, 2, 4, 2), ("z", "yl", "c", "x", "yh"))
    spec = P(DP, TENSOR)
    return jax.shard_map(
        local,
        mesh=finer,
        in_specs=(spec,) * 4,
        out_specs=(spec,) * 3,
        check_vma=False,
    )
```

```python
import jax
import jax.numpy as jnp
from jax import lax
from jax.experimental import pallas as pl
from jax.experimental.pallas import tpu as pltpu
from jax.sharding import Mesh
from jax.sharding import PartitionSpec as P

DP = ("z", "yl", "c")
TENSOR = ("x", "yh")
MESH = pl.DeviceIdType.MESH
F32 = jnp.float32
NEAR = (1, 15, 2)
FAR = (4, 12, 8)
DIRECT = (3,)
BLOCKS = (0, 3, 1, 2)
TOKENS = 1536
HALF = 768
B = 2048


def dot(a, b, dims):
    return lax.dot_general(a, b, (dims, ((), ())), preferred_element_type=F32)


def parts(v):
    high = v.astype(jnp.bfloat16)
    return high, (v - high.astype(F32)).astype(jnp.bfloat16)


def by_rows(a, b):
    over = ((1,), (1,))
    product = dot(a[0], b[0], over)
    for low in a[1:]:
        product = product + dot(low, b[0], over)
    for low in b[1:]:
        product = product + dot(a[0], low, over)
    return product


def by_columns(a, b):
    high, low = parts(a.T)
    over = ((1,), (0,))
    return dot(high, b[0], over) + (dot(low, b[0], over) + dot(high, b[1], over))


def total(v):
    return jnp.sum(jnp.sum(v * v, axis=1, keepdims=True), axis=0, keepdims=True)


def kernel(
    a_ref, o_ref, ls_ref, rs_ref, out_ref,
    a_own, o_own, a_in, o_in, part, c_in, c_sum, y_in, tile, z1_in, z1_sum, z2_in, grad, g_parts, gz, stat, rs_half,
    ls_in, hl, st, st_in, st_sum, qg, qg_in, ur, ur_in, la, turned, ub, u_half, uz, su, su_in, qu, qu_in,
    pr, pr_in, q_sum, qa, s_own, s1_in, s1_sum, s2_in,
    a_send, a_recv, send, recv, c_send, c_recv, y_send, y_recv, z_send, z_recv, z2_send, z2_recv,
    far_send, far_recv, near_send, near_recv, s_sems, relay,
):
    z, yl, c = lax.axis_index("z"), lax.axis_index("yl"), lax.axis_index("c")
    x, yh = lax.axis_index("x"), lax.axis_index("yh")
    zh, zb, z1 = z // 4, z % 2, (z // 2) % 2
    ylc = 2 * yl + c
    place = ylc * 8 + x * 2 + yh

    def at(**other):
        return {**dict(z=z, yl=yl, c=c, x=x, yh=yh), **other}

    def x_peer(k):
        return at(x=lax.rem(x + k, 4))

    def z_peer(k):
        return at(z=lax.rem(z + k, 16))

    def flip(n, bit):
        return n + bit - 2 * n * bit

    def y_peer(d, **other):
        return at(c=flip(c, d % 2), yl=flip(yl, d // 2 % 2), yh=flip(yh, d // 4), **other)

    bits = [(yh, 1 - yh), None, None, (c, 1 - c), (yl, 1 - yl)]
    xs = [flip(x % 2, k % 2) + 2 * flip(x // 2, k // 2) for k in range(4)]

    def plane_peer(d):
        return at(yh=bits[0][d % 2], x=xs[d // 2 % 4], c=bits[3][d // 8 % 2], yl=bits[4][d // 16])

    def remote(src, dst, s, r, peer):
        return pltpu.make_async_remote_copy(
            src_ref=src, dst_ref=dst, send_sem=s, recv_sem=r, device_id=peer, device_id_type=MESH
        )

    def settle(view, sem):
        pltpu.make_async_copy(view, view, sem).wait()

    drain = []

    def sent(view, sem):
        drain.append(lambda: settle(view, sem))

    barrier = pltpu.get_barrier_semaphore()

    def greet(peer):
        pl.semaphore_signal(barrier, inc=1, device_id=peer, device_id_type=MESH)

    copies = [
        pltpu.make_async_copy(a_ref, a_own, send.at[7]),
        pltpu.make_async_copy(o_ref, o_own, send.at[8]),
    ]
    for copy in copies:
        copy.start()
    for d in range(1, 32):
        greet(plane_peer(d))
    for k in (1, 2, 14, 15):
        greet(z_peer(k))
    pl.semaphore_wait(barrier, 31 + 4)

    def tell(n, k):
        pl.semaphore_signal(relay.at[n], inc=1, device_id=z_peer(k), device_id_type=MESH)

    remote(o_ref, o_in, send.at[11], recv.at[0], at(yh=1 - yh)).start()
    sent(o_in, send.at[11])
    sent(a_in, a_send)

    def rows(h):
        return pl.ds(h * HALF, HALF)

    for slot, k, h in ((0, 1, 0), (1, 3, 1), (0, 1, 1), (1, 3, 0)):
        remote(
            a_ref.at[rows(h)], a_in.at[slot, rows(h)], a_send, a_recv.at[slot, h], x_peer(k)
        ).start()

    for k in (1, 2, 14, 15):
        tell(0, k)

    own_cols = pl.ds(pl.multiple_of(yh * 256, 256), 256)
    other_cols = pl.ds(pl.multiple_of((1 - yh) * 256, 256), 256)

    def terms(k, own):
        acts = a_own[...] if k == 0 else a_in[k - 1]
        block = lax.dot_general(
            acts,
            o_own[...] if own else o_in[...],
            (((0,), (0,)), ((), ())),
            preferred_element_type=F32,
        )
        part[k, :, :, :, :, own_cols if own else other_cols] = block.reshape(2, 2, 2, 32, 256)

    def block_of(k):
        return lax.rem(x + BLOCKS[k], 4)

    def c_start(k):
        remote(part.at[k, :, :, 1 - c], c_in.at[k], c_send.at[k], c_recv.at[k], at(c=1 - c)).start()
        sent(c_in.at[k], c_send.at[k])

    def c_end(k):
        settle(c_in.at[k], c_recv.at[k])
        c_sum[k] = part[k, :, :, c] + c_in[k]
        remote(c_sum.at[k, :, 1 - yl], y_in.at[k], y_send.at[k], y_recv.at[k], at(yl=1 - yl)).start()
        sent(y_in.at[k], y_send.at[k])

    def half_of(zz):
        return pl.ds(pl.multiple_of(flip((zz // 2) % 2, yh) * 16, 16), 16)

    def y_end(k):
        settle(y_in.at[k], y_recv.at[k])
        tile[k] = c_sum[k, :, yl] + y_in[k]
        for i, step in enumerate(NEAR):
            m = lax.rem(z + step, 16)
            remote(
                tile.at[k, m % 2, half_of(m)], z1_in.at[k, i], z_send.at[k], z_recv.at[k], z_peer(step)
            ).start()
        sent(z1_in.at[k], z_send.at[k])

    mine = half_of(z)

    def columns_of(zz):
        return pl.ds(pl.multiple_of(zz * 128, 128), 128)

    def z1_end(k):
        settle(z1_in.at[k], z_recv.at[k])
        z1_sum[k] = tile[k, zb, mine] + z1_in[k, 0] + z1_in[k, 1] + z1_in[k, 2]
        if k in DIRECT:
            for i, step in enumerate(FAR):
                remote(z1_sum.at[k], z2_in.at[k, i], z2_send.at[k], z2_recv.at[k], z_peer(step)).start()
            sent(z2_in.at[k], z2_send.at[k])
            return
        for i, step in enumerate(FAR):
            at_zh = columns_of(lax.rem(zh + step // 4, 4))
            remote(
                z1_sum.at[k, :, at_zh], z2_in.at[k, i, :, at_zh], z2_send.at[k], z2_recv.at[k], z_peer(step)
            ).start()
        sent(z2_in.at[k, :, :, pl.ds(0, 128)], z2_send.at[k])

    def piece_of(k):
        return grad.at[block_of(k), zb, mine]

    def z2_own(k):
        if k in DIRECT:
            return
        settle(z2_in.at[k, :, :, pl.ds(0, 128)], z2_recv.at[k])
        cols = columns_of(zh)
        mine_k = grad.at[block_of(k), zb, mine, cols]
        mine_k[...] = z1_sum[k, :, cols] + (z2_in[k, 0, :, cols] + z2_in[k, 1, :, cols] + z2_in[k, 2, :, cols])
        for step in FAR:
            remote(mine_k, mine_k, far_send.at[k], far_recv.at[k], z_peer(step)).start()
        sent(z2_in.at[k, :, :, pl.ds(0, 128)], far_send.at[k])

    def z2_end(k):
        if k in DIRECT:
            settle(z2_in.at[k], z2_recv.at[k])
            piece_of(k)[...] = z1_sum[k] + (z2_in[k, 0] + z2_in[k, 1] + z2_in[k, 2])
        else:
            settle(z2_in.at[k, :, :, pl.ds(0, 128)], far_recv.at[k])
        for step in NEAR:
            remote(piece_of(k), piece_of(k), near_send.at[k], near_recv.at[k], z_peer(step)).start()
        sent(z2_in.at[k], near_send.at[k])

    def z3_end(k):
        settle(z2_in.at[k], near_recv.at[k])
        xb = block_of(k)
        high, low = parts(grad[xb].reshape(64, 512))
        g_parts[0, xb] = high
        g_parts[1, xb] = low

    rs_half[...] = rs_ref[...].astype(jnp.bfloat16)
    for copy in copies:
        copy.wait()
    terms(0, True)
    pl.semaphore_wait(relay.at[0], 4)
    for k in (3, 4, 12, 13):
        tell(1, k)
    settle(a_in.at[0, rows(0)], a_recv.at[0, 0])
    remote(a_in.at[0, rows(0)], a_in.at[2, rows(0)], a_send, a_recv.at[2, 0], x_peer(1)).start()
    settle(a_in.at[1, rows(1)], a_recv.at[1, 1])
    remote(a_in.at[1, rows(1)], a_in.at[2, rows(1)], a_send, a_recv.at[2, 1], x_peer(3)).start()
    pl.semaphore_wait(relay.at[1], 4)
    tell(2, 4)
    tell(2, 12)

    pl.semaphore_wait(relay.at[2], 2)

    stat_to = stat.at[zh, zb, :, pl.ds(pl.multiple_of(yh * 256, 256), 256)]
    for step in FAR:
        remote(rs_half, stat_to, send.at[1], recv.at[1], at(z=lax.rem(z + step, 16), yh=z1)).start()
    own_stat = remote(rs_half, stat_to, send.at[2], recv.at[1], at(yh=z1))
    pl.when(z1 == yh)(lambda: pltpu.make_async_copy(rs_half, stat_to, recv.at[1]).start())
    pl.when(z1 != yh)(lambda: own_stat.start())
    sent(stat.at[pl.ds(0, 3), 0, :, pl.ds(0, 256)], send.at[1])
    drain.append(lambda: pl.when(z1 != yh)(own_stat.wait_send))
    for b in range(2):
        zt = 4 * x + 2 * yh + b
        ls_from, ls_to = ls_ref.at[:, pl.ds(b * 128, 128)], ls_in.at[zh, zb]
        go = remote(ls_from, ls_to, send.at[3 + b], recv.at[2], at(z=zt, yh=z1))
        drain.append(lambda zt=zt, go=go: pl.when(zt != z)(go.wait_send))

        def keep(ls_from=ls_from, ls_to=ls_to):
            pltpu.make_async_copy(ls_from, ls_to, recv.at[2]).start()

        pl.when(zt == z)(keep)
        pl.when(zt != z)(go.start)

    settle(o_in, recv.at[0])
    terms(0, False)
    c_start(0)
    settle(a_in.at[0, rows(1)], a_recv.at[0, 1])
    terms(1, True)
    terms(1, False)
    c_start(1)

    @pl.when(z1 == yh)
    def _():
        view = stat.at[:, zb]
        settle(view, recv.at[1])
        for step in NEAR:
            remote(view, view, send.at[5], recv.at[3], z_peer(step)).start()

    drain.append(lambda: pl.when(z1 == yh)(lambda: settle(z2_in, send.at[5])))

    c_end(0)
    settle(a_in.at[1, rows(0)], a_recv.at[1, 0])
    terms(2, True)
    terms(2, False)
    c_start(2)
    c_end(1)
    c_end(2)
    y_end(0)

    settle(a_in.at[2, rows(0)], a_recv.at[2, 0])
    settle(a_in.at[2, rows(1)], a_recv.at[2, 1])
    terms(3, True)
    terms(3, False)
    c_start(3)

    @pl.when(x == zh)
    def _():
        settle(ls_in, recv.at[2])
        for k in range(1, 4):
            remote(ls_in, hl.at[1], send.at[6], recv.at[4], x_peer(k)).start()
        pltpu.make_async_copy(ls_in, hl.at[1], recv.at[4]).start()

    drain.append(lambda: pl.when(x == zh)(lambda: settle(st_in, send.at[6])))

    y_end(1)
    z1_end(0)
    c_end(3)
    y_end(2)
    z1_end(1)
    y_end(3)
    z1_end(2)
    z2_own(0)
    z1_end(3)
    z2_own(1)
    z2_own(2)
    z2_end(0)
    z2_end(1)
    z2_own(3)
    z2_end(2)
    z3_end(0)
    z2_end(3)

    home = 4 * zh + 2 * yh + zb
    gz_rows = gz.at[pl.ds(pl.multiple_of(ylc * 32 + flip(z1, yh) * 16, 16), 16)]
    piece = grad.at[zh, zb, mine]
    gz_other = gz.at[pl.ds(pl.multiple_of(ylc * 32 + 16, 16), 16)]
    gz_send = remote(piece, gz_rows, send.at[10], recv.at[21], at(z=home))

    @pl.when(home == z)
    def _():
        for d in range(1, 8):
            remote(piece, gz_rows, send.at[9], recv.at[6], y_peer(d)).start()
        pltpu.make_async_copy(piece, gz_rows, recv.at[6]).start()

    @pl.when(home != z)
    def _():
        gz_send.start()

    @pl.when(home == z)
    def _():
        settle(gz_other, recv.at[21])
        for d in range(1, 8):
            remote(gz_other, gz_other, send.at[18], recv.at[6], y_peer(d)).start()

    drain.append(lambda: pl.when(home != z)(gz_send.wait_send))
    drain.append(lambda: pl.when(home == z)(lambda: settle(gz.at[pl.ds(0, 112)], send.at[9])))
    drain.append(lambda: pl.when(home == z)(lambda: settle(gz.at[pl.ds(0, 112)], send.at[18])))
    z3_end(1)
    z3_end(2)
    z3_end(3)
    pl.when(home == z)(lambda: settle(gz.at[pl.ds(0, 112)], recv.at[6]))
    pl.when(home != z)(lambda: settle(gz, recv.at[6]))
    rows_z = parts(gz[...])

    def tile_of():
        return g_parts[0].reshape(256, 512), g_parts[1].reshape(256, 512)

    st[...] = by_rows(tile_of(), rows_z)
    for k in range(1, 4):
        remote(st, st_in.at[k - 1], send.at[14], recv.at[9], x_peer(k)).start()
    sent(st_in, send.at[14])

    @pl.when(x == zh)
    def _():
        cols = grad.at[:, :, :, pl.ds(pl.multiple_of(z % 4 * 128, 128), 128)]
        for k in range(1, 4):
            remote(cols, hl.at[0], send.at[13], recv.at[8], x_peer(k)).start()
        pltpu.make_async_copy(cols, hl.at[0], recv.at[8]).start()

    drain.append(lambda: pl.when(x == zh)(lambda: settle(st_in, send.at[13])))
    settle(hl.at[1], recv.at[4])
    settle(st_in, recv.at[9])
    st_sum[...] = st[...] + (st_in[0] + st_in[1] + st_in[2])
    lt = 0.9 * hl[1].reshape(256, 128) + 0.1 * st_sum[...]
    turned[...] = lt
    ur[0] = by_columns(lt, tile_of())

    def block_at(ref, d, *lead):
        r = pl.multiple_of((flip(c, d % 2) + 2 * flip(yl, d // 2 % 2)) * 32, 32)
        col = pl.multiple_of(flip(yh, d // 4) * 256, 256)
        return ref.at[(*lead, pl.ds(r, 32), pl.ds(col, 256))]

    for d in range(1, 8):
        remote(
            block_at(ur, d, 0), ur_in.at[0, d - 1], send.at[15], recv.at[10], y_peer(d)
        ).start()
    sent(ur_in.at[0], send.at[15])
    own = turned[pl.ds(pl.multiple_of(x * 64, 64), 64), :]
    la[ylc] = own
    for d in range(1, 4):
        remote(la.at[ylc], la.at[ylc], send.at[16], recv.at[11], y_peer(d)).start()
    sent(qg_in, send.at[16])
    lane = lax.broadcasted_iota(jnp.int32, (1, 128), 1)

    def sum_in_plane(n, values):
        v = jnp.zeros((1, 128), F32)
        for i, value in enumerate(values):
            v = jnp.where(lane == i, value, v)
        s_own[n] = v

        for d in range(1, 32):
            remote(s_own.at[n], s1_in.at[n, d - 1], s_sems.at[0, n], s_sems.at[1, n], plane_peer(d)).start()
        sent(s1_in.at[n], s_sems.at[0, n])

    def sum_along_z(n):
        settle(s1_in.at[n], s_sems.at[1, n])
        s1_sum[n] = s_own[n] + jnp.sum(s1_in[n], axis=0)

        for k in range(1, 16):
            remote(s1_sum.at[n], s2_in.at[n, k - 1], s_sems.at[2, n], s_sems.at[3, n], z_peer(k)).start()
        sent(s2_in.at[n], s_sems.at[2, n])

    def sums(n, count):
        settle(s2_in.at[n], s_sems.at[3, n])
        v = s1_sum[n] + jnp.sum(s2_in[n], axis=0)
        picked = [jnp.where(lane == i, v, 0.0) for i in range(count)]
        return [jnp.sum(p, axis=1, keepdims=True) for p in picked]

    settle(hl.at[0], recv.at[8])
    ur[1] = by_columns(hl[0].reshape(256, 128), tile_of())
    for d in range(1, 8):
        remote(
            block_at(ur, d, 1), ur_in.at[1, d - 1], send.at[0], recv.at[5], y_peer(d)
        ).start()
    drain.append(lambda: settle(ur_in.at[1], send.at[0]))
    sum_in_plane(0, (total(own), total(piece[...])))

    settle(ur_in.at[0], recv.at[10])
    u_block = block_at(ur, 0, 0)[...]
    for d in range(7):
        u_block = u_block + ur_in[0, d]
    ub[...] = u_block
    u_half[...] = u_block.astype(jnp.bfloat16)
    block_at(uz, 0)[...] = u_half[...]
    for d in range(1, 8):
        remote(u_half, block_at(uz, 0), send.at[17], recv.at[12], y_peer(d)).start()
    sent(uz.at[pl.ds(0, 112)], send.at[17])
    sum_along_z(0)

    settle(uz.at[pl.ds(0, 112)], recv.at[12])
    rows_u = (uz[...],)
    su[...] = by_rows(tile_of(), rows_u).astype(jnp.bfloat16)
    for k in range(1, 4):
        remote(su, su_in.at[k - 1], send.at[22], recv.at[17], x_peer(k)).start()
    sent(su_in, send.at[22])
    settle(ur_in.at[1], recv.at[5])
    r_block = block_at(ur, 0, 1)[...]
    for d in range(7):
        r_block = r_block + ur_in[1, d]
    right = 0.9 * rs_ref[...] + 0.1 * r_block
    out_ref[1] = right
    sum_in_plane(1, (total(right),))
    pl.when(z1 == yh)(lambda: settle(stat.at[:, 0], recv.at[3]))
    pl.when(z1 != yh)(lambda: settle(stat, recv.at[3]))
    qg[...] = by_rows((stat[...].reshape(256, 512),), rows_z).reshape(4, 64, 128)
    for k in range(1, 4):
        to = lax.rem(x + k, 4)
        remote(qg.at[to], qg_in.at[k - 1], send.at[12], recv.at[7], x_peer(k)).start()
    sent(qg_in, send.at[12])
    qu[...] = by_rows((stat[...].reshape(256, 512),), rows_u).astype(jnp.bfloat16).reshape(4, 64, 128)
    for k in range(1, 4):
        to = lax.rem(x + k, 4)
        remote(qu.at[to], qu_in.at[k - 1], send.at[23], recv.at[18], x_peer(k)).start()
    sent(qu_in, send.at[23])
    sum_along_z(1)

    def assembled(slots):
        v = slots[...].reshape(4, 2, 32, 128)
        whole = jnp.concatenate([v[i, b] for b in range(2) for i in range(4)], axis=0)
        return whole.T

    settle(la.at[pl.ds(0, 3)], recv.at[11])
    lt_rows = assembled(la)
    uz_rows = pl.ds(pl.multiple_of(ylc * 32, 32), 32)
    pr[:, 0:256] = lt_rows
    out_ref[0] = pr[uz_rows, 0:256]

    settle(su_in, recv.at[17])
    s_u = su[...].astype(F32)
    for i in range(3):
        s_u = s_u + su_in[i].astype(F32)
    settle(qg_in, recv.at[7])
    settle(qu_in, recv.at[18])
    left_total, grad_total = sums(0, 2)
    left_scale = jnp.sqrt(left_total / B + 1e-06)
    q_g = qg[x] + qg_in[0] + qg_in[1] + qg_in[2]
    q_u = qu[x].astype(F32)
    for i in range(3):
        q_u = q_u + qu_in[i].astype(F32)
    q_sum[...] = 0.9 * (5.0 * q_g - q_u / left_scale)
    qa[ylc] = q_sum[...]
    for d in range(1, 4):
        remote(q_sum, qa.at[ylc], send.at[24], recv.at[19], y_peer(d)).start()
    sent(qg_in, send.at[24])
    pr[...] = by_columns(0.1 * (5.0 * st_sum[...] - s_u / left_scale), tile_of())
    for d in range(1, 8):
        remote(block_at(pr, d), pr_in.at[d - 1], send.at[25], recv.at[20], y_peer(d)).start()
    sent(pr_in, send.at[25])
    pre_left = 5.0 * block_at(gz, 0)[...] - ub[...] / left_scale
    settle(qa.at[pl.ds(0, 3)], recv.at[19])
    turned[pl.ds(0, 128), :] = assembled(qa)[:, 0:128]
    turned[pl.ds(128, 128), :] = assembled(qa)[:, 128:256]
    low = turned[pl.ds(pl.multiple_of(ylc * 32, 32), 32), :]
    high = turned[pl.ds(pl.multiple_of(128 + ylc * 32, 32), 32), :]
    product = jnp.concatenate([low, high], axis=1) + block_at(pr, 0)[...]
    settle(pr_in, recv.at[20])
    for d in range(7):
        product = product + pr_in[d]
    (right_total,) = sums(1, 1)
    right_scale = jnp.sqrt(right_total / B + 1e-06)
    pre = 5.0 * pre_left - product / right_scale
    sum_in_plane(2, (total(pre),))
    sum_along_z(2)
    (pre_total,) = sums(2, 1)
    out_ref[2] = pre * (jnp.sqrt(grad_total + 1e-06) / jnp.sqrt(pre_total + 1e-06))

    for wait in drain:
        wait()


def local(activations, out_grads, left_stat, right_stat):
    vmem = pl.BlockSpec(memory_space=pltpu.VMEM)
    block = jax.ShapeDtypeStruct((32, 256), F32)
    bf16 = jnp.bfloat16
    shapes = [
        ((TOKENS, 256), bf16), ((TOKENS, 256), bf16),
        ((3, TOKENS, 256), bf16), ((TOKENS, 256), bf16),
        ((4, 2, 2, 2, 32, 512), F32), ((4, 2, 2, 32, 512), F32),
        ((4, 2, 2, 32, 512), F32), ((4, 2, 32, 512), F32),
        ((4, 2, 32, 512), F32), ((4, 3, 16, 512), F32),
        ((4, 16, 512), F32), ((4, 3, 16, 512), F32),
        ((4, 2, 32, 512), F32), ((2, 4, 64, 512), bf16), ((128, 512), F32),
        ((4, 2, 32, 512), bf16), ((32, 256), bf16),
        ((4, 2, 32, 128), F32), ((2, 4, 2, 32, 128), F32),
        ((256, 128), F32), ((3, 256, 128), F32), ((256, 128), F32),
        ((4, 64, 128), F32), ((3, 64, 128), F32),
        ((2, 128, 512), F32), ((2, 7, 32, 256), F32),
        ((4, 64, 128), F32), ((256, 128), F32), ((32, 256), F32), ((32, 256), bf16), ((128, 512), bf16),
        ((256, 128), bf16), ((3, 256, 128), bf16),
        ((4, 64, 128), bf16), ((3, 64, 128), bf16),
        ((128, 512), F32), ((7, 32, 256), F32),
        ((64, 128), F32), ((4, 64, 128), F32),
        ((3, 1, 128), F32), ((3, 31, 1, 128), F32),
        ((3, 1, 128), F32), ((3, 15, 1, 128), F32),
    ]
    dma = pltpu.SemaphoreType.DMA
    sems = [dma, dma((3, 2)), dma((26,)), dma((22,))] + [dma((4,))] * 12
    sems += [dma((4, 3)), pltpu.SemaphoreType.REGULAR((3,))]
    out = pl.pallas_call(
        kernel,
        out_shape=jax.ShapeDtypeStruct((3, 32, 256), F32),
        in_specs=[pl.BlockSpec(memory_space=pl.ANY)] * 2 + [vmem] * 2,
        out_specs=vmem,
        scratch_shapes=[pltpu.VMEM(s, d) for s, d in shapes] + sems,
        compiler_params=pltpu.CompilerParams(
            collective_id=0, has_side_effects=True, vmem_limit_bytes=60 * 2**20
        ),
        cost_estimate=pl.CostEstimate(flops=2 * 10**9, bytes_accessed=4 * 10**6, transcendentals=0),
    )(activations, out_grads, left_stat, right_stat)
    return out[0], out[1], out[2]


def solution(mesh):
    finer = Mesh(mesh.devices.reshape(16, 2, 2, 4, 2), ("z", "yl", "c", "x", "yh"))
    spec = P(DP, TENSOR)
    return jax.shard_map(
        local,
        mesh=finer,
        in_specs=(spec,) * 4,
        out_specs=(spec,) * 3,
        check_vma=False,
    )
```

```python
import jax
import jax.numpy as jnp
from jax import lax
from jax.experimental import pallas as pl
from jax.experimental.pallas import tpu as pltpu
from jax.sharding import Mesh
from jax.sharding import PartitionSpec as P

DP = ("z", "yl", "c")
TENSOR = ("x", "yh")
MESH = pl.DeviceIdType.MESH
F32 = jnp.float32
NEAR = (2, 1, 15)
FAR = (8, 4, 12)
ALONG_X = (2, 1, 3)
ALONG_Y = (4, 5, 6, 7, 2, 3, 1)
ALONG_Z = (8, 7, 9, 6, 10, 5, 11, 4, 12, 3, 13, 2, 14, 1, 15)
IN_PLANE = sorted(range(1, 32), key=lambda d: -((0, 1, 2, 1)[d // 2 % 4] + (0, 2, 1, 1)[d % 2 + d // 16 * 2]))
DIRECT = (3,)
BLOCKS = (0, 3, 1, 2)
TOKENS = 1536
HALF = 768
B = 2048


def dot(a, b, dims):
    return lax.dot_general(a, b, (dims, ((), ())), preferred_element_type=F32)


def parts(v):
    high = v.astype(jnp.bfloat16)
    return high, (v - high.astype(F32)).astype(jnp.bfloat16)


def by_rows(a, b):
    over = ((1,), (1,))
    product = dot(a[0], b[0], over)
    for low in a[1:]:
        product = product + dot(low, b[0], over)
    for low in b[1:]:
        product = product + dot(a[0], low, over)
    return product


def by_columns(a, b):
    high, low = parts(a.T)
    over = ((1,), (0,))
    return dot(high, b[0], over) + (dot(low, b[0], over) + dot(high, b[1], over))


def total(v):
    return jnp.sum(jnp.sum(v * v, axis=1, keepdims=True), axis=0, keepdims=True)


def kernel(
    a_ref, o_ref, ls_ref, rs_ref, out_ref,
    a_own, o_own, a_in, o_in, part, c_in, c_sum, y_in, tile, z1_in, z1_sum, z2_in, grad, g_parts, gz, stat, rs_half,
    ls_in, hl, st, st_in, st_sum, qg, qg_in, ur, ur_in, la, turned, ub, u_half, uz, su, su_in, qu, qu_in,
    pr, pr_in, q_sum, qa, s_own, s1_in, s1_sum, s2_in,
    a_send, a_recv, send, recv, c_send, c_recv, y_send, y_recv, z_send, z_recv, z2_send, z2_recv,
    far_send, far_recv, near_send, near_recv, s_sems, relay,
):
    z, yl, c = lax.axis_index("z"), lax.axis_index("yl"), lax.axis_index("c")
    x, yh = lax.axis_index("x"), lax.axis_index("yh")
    zh, zb, z1 = z // 4, z % 2, (z // 2) % 2
    ylc = 2 * yl + c
    place = ylc * 8 + x * 2 + yh

    def at(**other):
        return {**dict(z=z, yl=yl, c=c, x=x, yh=yh), **other}

    def x_peer(k):
        return at(x=lax.rem(x + k, 4))

    def z_peer(k):
        return at(z=lax.rem(z + k, 16))

    def flip(n, bit):
        return n + bit - 2 * n * bit

    def y_peer(d, **other):
        return at(c=flip(c, d % 2), yl=flip(yl, d // 2 % 2), yh=flip(yh, d // 4), **other)

    bits = [(yh, 1 - yh), None, None, (c, 1 - c), (yl, 1 - yl)]
    xs = [flip(x % 2, k % 2) + 2 * flip(x // 2, k // 2) for k in range(4)]

    def plane_peer(d):
        return at(yh=bits[0][d % 2], x=xs[d // 2 % 4], c=bits[3][d // 8 % 2], yl=bits[4][d // 16])

    def remote(src, dst, s, r, peer):
        return pltpu.make_async_remote_copy(
            src_ref=src, dst_ref=dst, send_sem=s, recv_sem=r, device_id=peer, device_id_type=MESH
        )

    def settle(view, sem):
        pltpu.make_async_copy(view, view, sem).wait()

    drain = []

    def sent(view, sem):
        drain.append(lambda: settle(view, sem))

    barrier = pltpu.get_barrier_semaphore()

    def greet(peer):
        pl.semaphore_signal(barrier, inc=1, device_id=peer, device_id_type=MESH)

    copies = [
        pltpu.make_async_copy(a_ref, a_own, send.at[7]),
        pltpu.make_async_copy(o_ref, o_own, send.at[8]),
    ]
    for copy in copies:
        copy.start()
    for d in range(1, 32):
        greet(plane_peer(d))
    for k in (1, 2, 14, 15):
        greet(z_peer(k))
    pl.semaphore_wait(barrier, 31 + 4)

    def tell(n, k):
        pl.semaphore_signal(relay.at[n], inc=1, device_id=z_peer(k), device_id_type=MESH)

    remote(o_ref, o_in, send.at[11], recv.at[0], at(yh=1 - yh)).start()
    sent(o_in, send.at[11])
    sent(a_in, a_send)

    def rows(h):
        return pl.ds(h * HALF, HALF)

    for slot, k, h in ((0, 1, 0), (1, 3, 1), (0, 1, 1), (1, 3, 0)):
        remote(
            a_ref.at[rows(h)], a_in.at[slot, rows(h)], a_send, a_recv.at[slot, h], x_peer(k)
        ).start()

    for k in (1, 2, 14, 15):
        tell(0, k)

    own_cols = pl.ds(pl.multiple_of(yh * 256, 256), 256)
    other_cols = pl.ds(pl.multiple_of((1 - yh) * 256, 256), 256)

    def terms(k, own):
        acts = a_own[...] if k == 0 else a_in[k - 1]
        block = lax.dot_general(
            acts,
            o_own[...] if own else o_in[...],
            (((0,), (0,)), ((), ())),
            preferred_element_type=F32,
        )
        part[k, :, :, :, :, own_cols if own else other_cols] = block.reshape(2, 2, 2, 32, 256)

    def block_of(k):
        return lax.rem(x + BLOCKS[k], 4)

    def c_start(k):
        remote(part.at[k, :, :, 1 - c], c_in.at[k], c_send.at[k], c_recv.at[k], at(c=1 - c)).start()
        sent(c_in.at[k], c_send.at[k])

    def c_end(k):
        settle(c_in.at[k], c_recv.at[k])
        c_sum[k] = part[k, :, :, c] + c_in[k]
        remote(c_sum.at[k, :, 1 - yl], y_in.at[k], y_send.at[k], y_recv.at[k], at(yl=1 - yl)).start()
        sent(y_in.at[k], y_send.at[k])

    def half_of(zz):
        return pl.ds(pl.multiple_of(flip((zz // 2) % 2, yh) * 16, 16), 16)

    def y_end(k):
        settle(y_in.at[k], y_recv.at[k])
        tile[k] = c_sum[k, :, yl] + y_in[k]
        for i, step in enumerate(NEAR):
            m = lax.rem(z + step, 16)
            remote(
                tile.at[k, m % 2, half_of(m)], z1_in.at[k, i], z_send.at[k], z_recv.at[k], z_peer(step)
            ).start()
        sent(z1_in.at[k], z_send.at[k])

    mine = half_of(z)

    def columns_of(zz):
        return pl.ds(pl.multiple_of(zz * 128, 128), 128)

    def z1_end(k):
        settle(z1_in.at[k], z_recv.at[k])
        z1_sum[k] = tile[k, zb, mine] + z1_in[k, 0] + z1_in[k, 1] + z1_in[k, 2]
        if k in DIRECT:
            for i, step in enumerate(FAR):
                remote(z1_sum.at[k], z2_in.at[k, i], z2_send.at[k], z2_recv.at[k], z_peer(step)).start()
            sent(z2_in.at[k], z2_send.at[k])
            return
        for i, step in enumerate(FAR):
            at_zh = columns_of(lax.rem(zh + step // 4, 4))
            remote(
                z1_sum.at[k, :, at_zh], z2_in.at[k, i, :, at_zh], z2_send.at[k], z2_recv.at[k], z_peer(step)
            ).start()
        sent(z2_in.at[k, :, :, pl.ds(0, 128)], z2_send.at[k])

    def piece_of(k):
        return grad.at[block_of(k), zb, mine]

    def z2_own(k):
        if k in DIRECT:
            return
        settle(z2_in.at[k, :, :, pl.ds(0, 128)], z2_recv.at[k])
        cols = columns_of(zh)
        mine_k = grad.at[block_of(k), zb, mine, cols]
        mine_k[...] = z1_sum[k, :, cols] + (z2_in[k, 0, :, cols] + z2_in[k, 1, :, cols] + z2_in[k, 2, :, cols])
        for step in FAR:
            remote(mine_k, mine_k, far_send.at[k], far_recv.at[k], z_peer(step)).start()
        sent(z2_in.at[k, :, :, pl.ds(0, 128)], far_send.at[k])

    def z2_end(k):
        if k in DIRECT:
            settle(z2_in.at[k], z2_recv.at[k])
            piece_of(k)[...] = z1_sum[k] + (z2_in[k, 0] + z2_in[k, 1] + z2_in[k, 2])
        else:
            settle(z2_in.at[k, :, :, pl.ds(0, 128)], far_recv.at[k])
        for step in NEAR:
            remote(piece_of(k), piece_of(k), near_send.at[k], near_recv.at[k], z_peer(step)).start()
        sent(z2_in.at[k], near_send.at[k])

    def z3_end(k):
        settle(z2_in.at[k], near_recv.at[k])
        xb = block_of(k)
        high, low = parts(grad[xb].reshape(64, 512))
        g_parts[0, xb] = high
        g_parts[1, xb] = low

    rs_half[...] = rs_ref[...].astype(jnp.bfloat16)
    for copy in copies:
        copy.wait()
    terms(0, True)
    pl.semaphore_wait(relay.at[0], 4)
    for k in (3, 4, 12, 13):
        tell(1, k)
    settle(a_in.at[0, rows(0)], a_recv.at[0, 0])
    remote(a_in.at[0, rows(0)], a_in.at[2, rows(0)], a_send, a_recv.at[2, 0], x_peer(1)).start()
    settle(a_in.at[1, rows(1)], a_recv.at[1, 1])
    remote(a_in.at[1, rows(1)], a_in.at[2, rows(1)], a_send, a_recv.at[2, 1], x_peer(3)).start()
    pl.semaphore_wait(relay.at[1], 4)
    tell(2, 4)
    tell(2, 12)

    pl.semaphore_wait(relay.at[2], 2)

    stat_to = stat.at[zh, zb, :, pl.ds(pl.multiple_of(yh * 256, 256), 256)]
    for step in FAR:
        remote(rs_half, stat_to, send.at[1], recv.at[1], at(z=lax.rem(z + step, 16), yh=z1)).start()
    own_stat = remote(rs_half, stat_to, send.at[2], recv.at[1], at(yh=z1))
    pl.when(z1 == yh)(lambda: pltpu.make_async_copy(rs_half, stat_to, recv.at[1]).start())
    pl.when(z1 != yh)(lambda: own_stat.start())
    sent(stat.at[pl.ds(0, 3), 0, :, pl.ds(0, 256)], send.at[1])
    drain.append(lambda: pl.when(z1 != yh)(own_stat.wait_send))
    for b in range(2):
        zt = 4 * x + 2 * yh + b
        ls_from, ls_to = ls_ref.at[:, pl.ds(b * 128, 128)], ls_in.at[zh, zb]
        go = remote(ls_from, ls_to, send.at[3 + b], recv.at[2], at(z=zt, yh=z1))
        drain.append(lambda zt=zt, go=go: pl.when(zt != z)(go.wait_send))

        def keep(ls_from=ls_from, ls_to=ls_to):
            pltpu.make_async_copy(ls_from, ls_to, recv.at[2]).start()

        pl.when(zt == z)(keep)
        pl.when(zt != z)(go.start)

    settle(o_in, recv.at[0])
    terms(0, False)
    c_start(0)
    settle(a_in.at[0, rows(1)], a_recv.at[0, 1])
    terms(1, True)
    terms(1, False)
    c_start(1)

    @pl.when(z1 == yh)
    def _():
        view = stat.at[:, zb]
        settle(view, recv.at[1])
        for step in NEAR:
            remote(view, view, send.at[5], recv.at[3], z_peer(step)).start()

    drain.append(lambda: pl.when(z1 == yh)(lambda: settle(z2_in, send.at[5])))

    c_end(0)
    settle(a_in.at[1, rows(0)], a_recv.at[1, 0])
    terms(2, True)
    terms(2, False)
    c_start(2)
    c_end(1)
    c_end(2)
    y_end(0)

    settle(a_in.at[2, rows(0)], a_recv.at[2, 0])
    settle(a_in.at[2, rows(1)], a_recv.at[2, 1])
    terms(3, True)
    terms(3, False)
    c_start(3)

    @pl.when(x == zh)
    def _():
        settle(ls_in, recv.at[2])
        for k in ALONG_X:
            remote(ls_in, hl.at[1], send.at[6], recv.at[4], x_peer(k)).start()
        pltpu.make_async_copy(ls_in, hl.at[1], recv.at[4]).start()

    drain.append(lambda: pl.when(x == zh)(lambda: settle(st_in, send.at[6])))

    y_end(1)
    z1_end(0)
    c_end(3)
    y_end(2)
    z1_end(1)
    y_end(3)
    z1_end(2)
    z2_own(0)
    z1_end(3)
    z2_own(1)
    z2_own(2)
    z2_end(0)
    z2_end(1)
    z2_own(3)
    z2_end(2)
    z3_end(0)
    z2_end(3)

    home = 4 * zh + 2 * yh + zb
    gz_rows = gz.at[pl.ds(pl.multiple_of(ylc * 32 + flip(z1, yh) * 16, 16), 16)]
    piece = grad.at[zh, zb, mine]
    gz_other = gz.at[pl.ds(pl.multiple_of(ylc * 32 + 16, 16), 16)]
    gz_send = remote(piece, gz_rows, send.at[10], recv.at[21], at(z=home))

    @pl.when(home == z)
    def _():
        for d in ALONG_Y:
            remote(piece, gz_rows, send.at[9], recv.at[6], y_peer(d)).start()
        pltpu.make_async_copy(piece, gz_rows, recv.at[6]).start()

    @pl.when(home != z)
    def _():
        gz_send.start()

    @pl.when(home == z)
    def _():
        settle(gz_other, recv.at[21])
        for d in ALONG_Y:
            remote(gz_other, gz_other, send.at[18], recv.at[6], y_peer(d)).start()

    drain.append(lambda: pl.when(home != z)(gz_send.wait_send))
    drain.append(lambda: pl.when(home == z)(lambda: settle(gz.at[pl.ds(0, 112)], send.at[9])))
    drain.append(lambda: pl.when(home == z)(lambda: settle(gz.at[pl.ds(0, 112)], send.at[18])))
    z3_end(1)
    z3_end(2)
    z3_end(3)
    pl.when(home == z)(lambda: settle(gz.at[pl.ds(0, 112)], recv.at[6]))
    pl.when(home != z)(lambda: settle(gz, recv.at[6]))
    rows_z = parts(gz[...])

    def tile_of():
        return g_parts[0].reshape(256, 512), g_parts[1].reshape(256, 512)

    st[...] = by_rows(tile_of(), rows_z)
    for k in ALONG_X:
        remote(st, st_in.at[k - 1], send.at[14], recv.at[9], x_peer(k)).start()
    sent(st_in, send.at[14])

    @pl.when(x == zh)
    def _():
        cols = grad.at[:, :, :, pl.ds(pl.multiple_of(z % 4 * 128, 128), 128)]
        for k in ALONG_X:
            remote(cols, hl.at[0], send.at[13], recv.at[8], x_peer(k)).start()
        pltpu.make_async_copy(cols, hl.at[0], recv.at[8]).start()

    drain.append(lambda: pl.when(x == zh)(lambda: settle(st_in, send.at[13])))
    settle(hl.at[1], recv.at[4])
    settle(st_in, recv.at[9])
    st_sum[...] = st[...] + (st_in[0] + st_in[1] + st_in[2])
    lt = 0.9 * hl[1].reshape(256, 128) + 0.1 * st_sum[...]
    turned[...] = lt
    ur[0] = by_columns(lt, tile_of())

    def block_at(ref, d, *lead):
        r = pl.multiple_of((flip(c, d % 2) + 2 * flip(yl, d // 2 % 2)) * 32, 32)
        col = pl.multiple_of(flip(yh, d // 4) * 256, 256)
        return ref.at[(*lead, pl.ds(r, 32), pl.ds(col, 256))]

    for d in ALONG_Y:
        remote(
            block_at(ur, d, 0), ur_in.at[0, d - 1], send.at[15], recv.at[10], y_peer(d)
        ).start()
    sent(ur_in.at[0], send.at[15])
    own = turned[pl.ds(pl.multiple_of(x * 64, 64), 64), :]
    la[ylc] = own
    for d in range(1, 4):
        remote(la.at[ylc], la.at[ylc], send.at[16], recv.at[11], y_peer(d)).start()
    sent(qg_in, send.at[16])
    lane = lax.broadcasted_iota(jnp.int32, (1, 128), 1)

    def sum_in_plane(n, values):
        v = jnp.zeros((1, 128), F32)
        for i, value in enumerate(values):
            v = jnp.where(lane == i, value, v)
        s_own[n] = v

        for d in IN_PLANE:
            remote(s_own.at[n], s1_in.at[n, d - 1], s_sems.at[0, n], s_sems.at[1, n], plane_peer(d)).start()
        sent(s1_in.at[n], s_sems.at[0, n])

    def sum_along_z(n):
        settle(s1_in.at[n], s_sems.at[1, n])
        s1_sum[n] = s_own[n] + jnp.sum(s1_in[n], axis=0)

        for k in ALONG_Z:
            remote(s1_sum.at[n], s2_in.at[n, k - 1], s_sems.at[2, n], s_sems.at[3, n], z_peer(k)).start()
        sent(s2_in.at[n], s_sems.at[2, n])

    def sums(n, count):
        settle(s2_in.at[n], s_sems.at[3, n])
        v = s1_sum[n] + jnp.sum(s2_in[n], axis=0)
        picked = [jnp.where(lane == i, v, 0.0) for i in range(count)]
        return [jnp.sum(p, axis=1, keepdims=True) for p in picked]

    settle(hl.at[0], recv.at[8])
    ur[1] = by_columns(hl[0].reshape(256, 128), tile_of())
    for d in ALONG_Y:
        remote(
            block_at(ur, d, 1), ur_in.at[1, d - 1], send.at[0], recv.at[5], y_peer(d)
        ).start()
    drain.append(lambda: settle(ur_in.at[1], send.at[0]))
    sum_in_plane(0, (total(own), total(piece[...])))

    settle(ur_in.at[0], recv.at[10])
    u_block = block_at(ur, 0, 0)[...]
    for d in range(7):
        u_block = u_block + ur_in[0, d]
    ub[...] = u_block
    u_half[...] = u_block.astype(jnp.bfloat16)
    block_at(uz, 0)[...] = u_half[...]
    for d in ALONG_Y:
        remote(u_half, block_at(uz, 0), send.at[17], recv.at[12], y_peer(d)).start()
    sent(uz.at[pl.ds(0, 112)], send.at[17])
    sum_along_z(0)

    settle(uz.at[pl.ds(0, 112)], recv.at[12])
    rows_u = (uz[...],)
    su[...] = by_rows(tile_of(), rows_u).astype(jnp.bfloat16)
    for k in ALONG_X:
        remote(su, su_in.at[k - 1], send.at[22], recv.at[17], x_peer(k)).start()
    sent(su_in, send.at[22])
    settle(ur_in.at[1], recv.at[5])
    r_block = block_at(ur, 0, 1)[...]
    for d in range(7):
        r_block = r_block + ur_in[1, d]
    right = 0.9 * rs_ref[...] + 0.1 * r_block
    out_ref[1] = right
    sum_in_plane(1, (total(right),))
    pl.when(z1 == yh)(lambda: settle(stat.at[:, 0], recv.at[3]))
    pl.when(z1 != yh)(lambda: settle(stat, recv.at[3]))
    qg[...] = by_rows((stat[...].reshape(256, 512),), rows_z).reshape(4, 64, 128)
    for k in ALONG_X:
        to = lax.rem(x + k, 4)
        remote(qg.at[to], qg_in.at[k - 1], send.at[12], recv.at[7], x_peer(k)).start()
    sent(qg_in, send.at[12])
    qu[...] = by_rows((stat[...].reshape(256, 512),), rows_u).astype(jnp.bfloat16).reshape(4, 64, 128)
    for k in ALONG_X:
        to = lax.rem(x + k, 4)
        remote(qu.at[to], qu_in.at[k - 1], send.at[23], recv.at[18], x_peer(k)).start()
    sent(qu_in, send.at[23])
    sum_along_z(1)

    def assembled(slots):
        v = slots[...].reshape(4, 2, 32, 128)
        whole = jnp.concatenate([v[i, b] for b in range(2) for i in range(4)], axis=0)
        return whole.T

    settle(la.at[pl.ds(0, 3)], recv.at[11])
    lt_rows = assembled(la)
    uz_rows = pl.ds(pl.multiple_of(ylc * 32, 32), 32)
    pr[:, 0:256] = lt_rows
    out_ref[0] = pr[uz_rows, 0:256]

    settle(su_in, recv.at[17])
    s_u = su[...].astype(F32)
    for i in range(3):
        s_u = s_u + su_in[i].astype(F32)
    settle(qg_in, recv.at[7])
    settle(qu_in, recv.at[18])
    left_total, grad_total = sums(0, 2)
    left_scale = jnp.sqrt(left_total / B + 1e-06)
    q_g = qg[x] + qg_in[0] + qg_in[1] + qg_in[2]
    q_u = qu[x].astype(F32)
    for i in range(3):
        q_u = q_u + qu_in[i].astype(F32)
    q_sum[...] = 0.9 * (5.0 * q_g - q_u / left_scale)
    qa[ylc] = q_sum[...]
    for d in range(1, 4):
        remote(q_sum, qa.at[ylc], send.at[24], recv.at[19], y_peer(d)).start()
    sent(qg_in, send.at[24])
    pr[...] = by_columns(0.1 * (5.0 * st_sum[...] - s_u / left_scale), tile_of())
    for d in ALONG_Y:
        remote(block_at(pr, d), pr_in.at[d - 1], send.at[25], recv.at[20], y_peer(d)).start()
    sent(pr_in, send.at[25])
    pre_left = 5.0 * block_at(gz, 0)[...] - ub[...] / left_scale
    settle(qa.at[pl.ds(0, 3)], recv.at[19])
    turned[pl.ds(0, 128), :] = assembled(qa)[:, 0:128]
    turned[pl.ds(128, 128), :] = assembled(qa)[:, 128:256]
    low = turned[pl.ds(pl.multiple_of(ylc * 32, 32), 32), :]
    high = turned[pl.ds(pl.multiple_of(128 + ylc * 32, 32), 32), :]
    product = jnp.concatenate([low, high], axis=1) + block_at(pr, 0)[...]
    settle(pr_in, recv.at[20])
    for d in range(7):
        product = product + pr_in[d]
    (right_total,) = sums(1, 1)
    right_scale = jnp.sqrt(right_total / B + 1e-06)
    pre = 5.0 * pre_left - product / right_scale
    sum_in_plane(2, (total(pre),))
    sum_along_z(2)
    (pre_total,) = sums(2, 1)
    out_ref[2] = pre * (jnp.sqrt(grad_total + 1e-06) / jnp.sqrt(pre_total + 1e-06))

    for wait in drain:
        wait()


def local(activations, out_grads, left_stat, right_stat):
    vmem = pl.BlockSpec(memory_space=pltpu.VMEM)
    block = jax.ShapeDtypeStruct((32, 256), F32)
    bf16 = jnp.bfloat16
    shapes = [
        ((TOKENS, 256), bf16), ((TOKENS, 256), bf16),
        ((3, TOKENS, 256), bf16), ((TOKENS, 256), bf16),
        ((4, 2, 2, 2, 32, 512), F32), ((4, 2, 2, 32, 512), F32),
        ((4, 2, 2, 32, 512), F32), ((4, 2, 32, 512), F32),
        ((4, 2, 32, 512), F32), ((4, 3, 16, 512), F32),
        ((4, 16, 512), F32), ((4, 3, 16, 512), F32),
        ((4, 2, 32, 512), F32), ((2, 4, 64, 512), bf16), ((128, 512), F32),
        ((4, 2, 32, 512), bf16), ((32, 256), bf16),
        ((4, 2, 32, 128), F32), ((2, 4, 2, 32, 128), F32),
        ((256, 128), F32), ((3, 256, 128), F32), ((256, 128), F32),
        ((4, 64, 128), F32), ((3, 64, 128), F32),
        ((2, 128, 512), F32), ((2, 7, 32, 256), F32),
        ((4, 64, 128), F32), ((256, 128), F32), ((32, 256), F32), ((32, 256), bf16), ((128, 512), bf16),
        ((256, 128), bf16), ((3, 256, 128), bf16),
        ((4, 64, 128), bf16), ((3, 64, 128), bf16),
        ((128, 512), F32), ((7, 32, 256), F32),
        ((64, 128), F32), ((4, 64, 128), F32),
        ((3, 1, 128), F32), ((3, 31, 1, 128), F32),
        ((3, 1, 128), F32), ((3, 15, 1, 128), F32),
    ]
    dma = pltpu.SemaphoreType.DMA
    sems = [dma, dma((3, 2)), dma((26,)), dma((22,))] + [dma((4,))] * 12
    sems += [dma((4, 3)), pltpu.SemaphoreType.REGULAR((3,))]
    out = pl.pallas_call(
        kernel,
        out_shape=jax.ShapeDtypeStruct((3, 32, 256), F32),
        in_specs=[pl.BlockSpec(memory_space=pl.ANY)] * 2 + [vmem] * 2,
        out_specs=vmem,
        scratch_shapes=[pltpu.VMEM(s, d) for s, d in shapes] + sems,
        compiler_params=pltpu.CompilerParams(
            collective_id=0, has_side_effects=True, vmem_limit_bytes=60 * 2**20
        ),
        cost_estimate=pl.CostEstimate(flops=2 * 10**9, bytes_accessed=4 * 10**6, transcendentals=0),
    )(activations, out_grads, left_stat, right_stat)
    return out[0], out[1], out[2]


def solution(mesh):
    finer = Mesh(mesh.devices.reshape(16, 2, 2, 4, 2), ("z", "yl", "c", "x", "yh"))
    spec = P(DP, TENSOR)
    return jax.shard_map(
        local,
        mesh=finer,
        in_specs=(spec,) * 4,
        out_specs=(spec,) * 3,
        check_vma=False,
    )
```

```python
import jax
import jax.numpy as jnp
from jax import lax
from jax.experimental import pallas as pl
from jax.experimental.pallas import tpu as pltpu
from jax.sharding import Mesh
from jax.sharding import PartitionSpec as P

DP = ("z", "yl", "c")
TENSOR = ("x", "yh")
MESH = pl.DeviceIdType.MESH
F32 = jnp.float32
NEAR = (2, 1, 15)
FAR = (8, 4, 12)
ALONG_X = (2, 1, 3)
ALONG_Y = (4, 5, 6, 7, 2, 3, 1)
ALONG_Z = (8, 7, 9, 6, 10, 5, 11, 4, 12, 3, 13, 2, 14, 1, 15)
IN_PLANE = sorted(range(1, 32), key=lambda d: -((0, 1, 2, 1)[d // 2 % 4] + (0, 2, 1, 1)[d % 2 + d // 16 * 2]))
DIRECT = (3,)
BLOCKS = (0, 3, 1, 2)
TOKENS = 1536
HALF = 768
B = 2048


def dot(a, b, dims):
    return lax.dot_general(a, b, (dims, ((), ())), preferred_element_type=F32)


def parts(v):
    high = v.astype(jnp.bfloat16)
    return high, (v - high.astype(F32)).astype(jnp.bfloat16)


def by_rows(a, b):
    over = ((1,), (1,))
    product = dot(a[0], b[0], over)
    for low in a[1:]:
        product = product + dot(low, b[0], over)
    for low in b[1:]:
        product = product + dot(a[0], low, over)
    return product


def by_columns(a, b):
    high, low = parts(a.T)
    over = ((1,), (0,))
    return dot(high, b[0], over) + (dot(low, b[0], over) + dot(high, b[1], over))


def total(v):
    return jnp.sum(jnp.sum(v * v, axis=1, keepdims=True), axis=0, keepdims=True)


def kernel(
    a_ref, o_ref, ls_hbm, rs_hbm, out_ref,
    a_own, o_own, ls_ref, rs_ref, a_in, o_in, part, c_in, c_sum, y_in, tile, z1_in, z1_sum, z2_in, grad, g_parts, gz, stat, rs_half,
    ls_in, hl, st, st_in, st_sum, qg, qg_in, ur, ur_in, la, turned, ub, u_half, uz, su, su_in, qu, qu_in,
    pr, pr_in, q_sum, qa, s_own, s1_in, s1_sum, s2_in,
    a_send, a_recv, send, recv, c_send, c_recv, y_send, y_recv, z_send, z_recv, z2_send, z2_recv,
    far_send, far_recv, near_send, near_recv, s_sems, relay,
):
    z, yl, c = lax.axis_index("z"), lax.axis_index("yl"), lax.axis_index("c")
    x, yh = lax.axis_index("x"), lax.axis_index("yh")
    zh, zb, z1 = z // 4, z % 2, (z // 2) % 2
    ylc = 2 * yl + c
    place = ylc * 8 + x * 2 + yh

    def at(**other):
        return {**dict(z=z, yl=yl, c=c, x=x, yh=yh), **other}

    def x_peer(k):
        return at(x=lax.rem(x + k, 4))

    def z_peer(k):
        return at(z=lax.rem(z + k, 16))

    def flip(n, bit):
        return n + bit - 2 * n * bit

    def y_peer(d, **other):
        return at(c=flip(c, d % 2), yl=flip(yl, d // 2 % 2), yh=flip(yh, d // 4), **other)

    bits = [(yh, 1 - yh), None, None, (c, 1 - c), (yl, 1 - yl)]
    xs = [flip(x % 2, k % 2) + 2 * flip(x // 2, k // 2) for k in range(4)]

    def plane_peer(d):
        return at(yh=bits[0][d % 2], x=xs[d // 2 % 4], c=bits[3][d // 8 % 2], yl=bits[4][d // 16])

    def remote(src, dst, s, r, peer):
        return pltpu.make_async_remote_copy(
            src_ref=src, dst_ref=dst, send_sem=s, recv_sem=r, device_id=peer, device_id_type=MESH
        )

    def settle(view, sem):
        pltpu.make_async_copy(view, view, sem).wait()

    drain = []

    def sent(view, sem):
        drain.append(lambda: settle(view, sem))

    barrier = pltpu.get_barrier_semaphore()

    def greet(peer):
        pl.semaphore_signal(barrier, inc=1, device_id=peer, device_id_type=MESH)

    copies = [
        pltpu.make_async_copy(a_ref, a_own, send.at[7]),
        pltpu.make_async_copy(o_ref, o_own, send.at[8]),
        pltpu.make_async_copy(ls_hbm, ls_ref, send.at[20]),
        pltpu.make_async_copy(rs_hbm, rs_ref, send.at[21]),
    ]
    for copy in copies:
        copy.start()
    for d in range(1, 32):
        greet(plane_peer(d))
    for k in (1, 2, 14, 15):
        greet(z_peer(k))
    pl.semaphore_wait(barrier, 31 + 4)

    def tell(n, k):
        pl.semaphore_signal(relay.at[n], inc=1, device_id=z_peer(k), device_id_type=MESH)

    remote(o_ref, o_in, send.at[11], recv.at[0], at(yh=1 - yh)).start()
    sent(o_in, send.at[11])
    sent(a_in, a_send)

    def rows(h):
        return pl.ds(h * HALF, HALF)

    for slot, k, h in ((0, 1, 0), (1, 3, 1), (0, 1, 1), (1, 3, 0)):
        remote(
            a_ref.at[rows(h)], a_in.at[slot, rows(h)], a_send, a_recv.at[slot, h], x_peer(k)
        ).start()

    for k in (1, 2, 14, 15):
        tell(0, k)

    own_cols = pl.ds(pl.multiple_of(yh * 256, 256), 256)
    other_cols = pl.ds(pl.multiple_of((1 - yh) * 256, 256), 256)

    def terms(k, own):
        acts = a_own[...] if k == 0 else a_in[k - 1]
        block = lax.dot_general(
            acts,
            o_own[...] if own else o_in[...],
            (((0,), (0,)), ((), ())),
            preferred_element_type=F32,
        )
        part[k, :, :, :, :, own_cols if own else other_cols] = block.reshape(2, 2, 2, 32, 256)

    def block_of(k):
        return lax.rem(x + BLOCKS[k], 4)

    def c_start(k):
        remote(part.at[k, :, :, 1 - c], c_in.at[k], c_send.at[k], c_recv.at[k], at(c=1 - c)).start()
        sent(c_in.at[k], c_send.at[k])

    def c_end(k):
        settle(c_in.at[k], c_recv.at[k])
        c_sum[k] = part[k, :, :, c] + c_in[k]
        remote(c_sum.at[k, :, 1 - yl], y_in.at[k], y_send.at[k], y_recv.at[k], at(yl=1 - yl)).start()
        sent(y_in.at[k], y_send.at[k])

    def half_of(zz):
        return pl.ds(pl.multiple_of(flip((zz // 2) % 2, yh) * 16, 16), 16)

    def y_end(k):
        settle(y_in.at[k], y_recv.at[k])
        tile[k] = c_sum[k, :, yl] + y_in[k]
        for i, step in enumerate(NEAR):
            m = lax.rem(z + step, 16)
            remote(
                tile.at[k, m % 2, half_of(m)], z1_in.at[k, i], z_send.at[k], z_recv.at[k], z_peer(step)
            ).start()
        sent(z1_in.at[k], z_send.at[k])

    mine = half_of(z)

    def columns_of(zz):
        return pl.ds(pl.multiple_of(zz * 128, 128), 128)

    def z1_end(k):
        settle(z1_in.at[k], z_recv.at[k])
        z1_sum[k] = tile[k, zb, mine] + z1_in[k, 0] + z1_in[k, 1] + z1_in[k, 2]
        if k in DIRECT:
            for i, step in enumerate(FAR):
                remote(z1_sum.at[k], z2_in.at[k, i], z2_send.at[k], z2_recv.at[k], z_peer(step)).start()
            sent(z2_in.at[k], z2_send.at[k])
            return
        for i, step in enumerate(FAR):
            at_zh = columns_of(lax.rem(zh + step // 4, 4))
            remote(
                z1_sum.at[k, :, at_zh], z2_in.at[k, i, :, at_zh], z2_send.at[k], z2_recv.at[k], z_peer(step)
            ).start()
        sent(z2_in.at[k, :, :, pl.ds(0, 128)], z2_send.at[k])

    def piece_of(k):
        return grad.at[block_of(k), zb, mine]

    def z2_own(k):
        if k in DIRECT:
            return
        settle(z2_in.at[k, :, :, pl.ds(0, 128)], z2_recv.at[k])
        cols = columns_of(zh)
        mine_k = grad.at[block_of(k), zb, mine, cols]
        mine_k[...] = z1_sum[k, :, cols] + (z2_in[k, 0, :, cols] + z2_in[k, 1, :, cols] + z2_in[k, 2, :, cols])
        for step in FAR:
            remote(mine_k, mine_k, far_send.at[k], far_recv.at[k], z_peer(step)).start()
        sent(z2_in.at[k, :, :, pl.ds(0, 128)], far_send.at[k])

    def z2_end(k):
        if k in DIRECT:
            settle(z2_in.at[k], z2_recv.at[k])
            piece_of(k)[...] = z1_sum[k] + (z2_in[k, 0] + z2_in[k, 1] + z2_in[k, 2])
        else:
            settle(z2_in.at[k, :, :, pl.ds(0, 128)], far_recv.at[k])
        for step in NEAR:
            remote(piece_of(k), piece_of(k), near_send.at[k], near_recv.at[k], z_peer(step)).start()
        sent(z2_in.at[k], near_send.at[k])

    def z3_end(k):
        settle(z2_in.at[k], near_recv.at[k])
        xb = block_of(k)
        high, low = parts(grad[xb].reshape(64, 512))
        g_parts[0, xb] = high
        g_parts[1, xb] = low

    for copy in copies:
        copy.wait()
    rs_half[...] = rs_ref[...].astype(jnp.bfloat16)
    terms(0, True)
    pl.semaphore_wait(relay.at[0], 4)
    for k in (3, 4, 12, 13):
        tell(1, k)
    settle(a_in.at[0, rows(0)], a_recv.at[0, 0])
    remote(a_in.at[0, rows(0)], a_in.at[2, rows(0)], a_send, a_recv.at[2, 0], x_peer(1)).start()
    settle(a_in.at[1, rows(1)], a_recv.at[1, 1])
    remote(a_in.at[1, rows(1)], a_in.at[2, rows(1)], a_send, a_recv.at[2, 1], x_peer(3)).start()
    pl.semaphore_wait(relay.at[1], 4)
    tell(2, 4)
    tell(2, 12)

    pl.semaphore_wait(relay.at[2], 2)

    stat_to = stat.at[zh, zb, :, pl.ds(pl.multiple_of(yh * 256, 256), 256)]
    for step in FAR:
        remote(rs_half, stat_to, send.at[1], recv.at[1], at(z=lax.rem(z + step, 16), yh=z1)).start()
    own_stat = remote(rs_half, stat_to, send.at[2], recv.at[1], at(yh=z1))
    pl.when(z1 == yh)(lambda: pltpu.make_async_copy(rs_half, stat_to, recv.at[1]).start())
    pl.when(z1 != yh)(lambda: own_stat.start())
    sent(stat.at[pl.ds(0, 3), 0, :, pl.ds(0, 256)], send.at[1])
    drain.append(lambda: pl.when(z1 != yh)(own_stat.wait_send))
    for b in range(2):
        zt = 4 * x + 2 * yh + b
        ls_from, ls_to = ls_ref.at[:, pl.ds(b * 128, 128)], ls_in.at[zh, zb]
        go = remote(ls_from, ls_to, send.at[3 + b], recv.at[2], at(z=zt, yh=z1))
        drain.append(lambda zt=zt, go=go: pl.when(zt != z)(go.wait_send))

        def keep(ls_from=ls_from, ls_to=ls_to):
            pltpu.make_async_copy(ls_from, ls_to, recv.at[2]).start()

        pl.when(zt == z)(keep)
        pl.when(zt != z)(go.start)

    settle(o_in, recv.at[0])
    terms(0, False)
    c_start(0)
    settle(a_in.at[0, rows(1)], a_recv.at[0, 1])
    terms(1, True)
    terms(1, False)
    c_start(1)

    @pl.when(z1 == yh)
    def _():
        view = stat.at[:, zb]
        settle(view, recv.at[1])
        for step in NEAR:
            remote(view, view, send.at[5], recv.at[3], z_peer(step)).start()

    drain.append(lambda: pl.when(z1 == yh)(lambda: settle(z2_in, send.at[5])))

    c_end(0)
    settle(a_in.at[1, rows(0)], a_recv.at[1, 0])
    terms(2, True)
    terms(2, False)
    c_start(2)
    c_end(1)
    c_end(2)
    y_end(0)

    settle(a_in.at[2, rows(0)], a_recv.at[2, 0])
    settle(a_in.at[2, rows(1)], a_recv.at[2, 1])
    terms(3, True)
    terms(3, False)
    c_start(3)

    @pl.when(x == zh)
    def _():
        settle(ls_in, recv.at[2])
        for k in ALONG_X:
            remote(ls_in, hl.at[1], send.at[6], recv.at[4], x_peer(k)).start()
        pltpu.make_async_copy(ls_in, hl.at[1], recv.at[4]).start()

    drain.append(lambda: pl.when(x == zh)(lambda: settle(st_in, send.at[6])))

    y_end(1)
    z1_end(0)
    c_end(3)
    y_end(2)
    z1_end(1)
    y_end(3)
    z1_end(2)
    z2_own(0)
    z1_end(3)
    z2_own(1)
    z2_own(2)
    z2_end(0)
    z2_end(1)
    z2_own(3)
    z2_end(2)
    z3_end(0)
    z2_end(3)

    home = 4 * zh + 2 * yh + zb
    gz_rows = gz.at[pl.ds(pl.multiple_of(ylc * 32 + flip(z1, yh) * 16, 16), 16)]
    piece = grad.at[zh, zb, mine]
    gz_other = gz.at[pl.ds(pl.multiple_of(ylc * 32 + 16, 16), 16)]
    gz_send = remote(piece, gz_rows, send.at[10], recv.at[21], at(z=home))

    @pl.when(home == z)
    def _():
        for d in ALONG_Y:
            remote(piece, gz_rows, send.at[9], recv.at[6], y_peer(d)).start()
        pltpu.make_async_copy(piece, gz_rows, recv.at[6]).start()

    @pl.when(home != z)
    def _():
        gz_send.start()

    @pl.when(home == z)
    def _():
        settle(gz_other, recv.at[21])
        for d in ALONG_Y:
            remote(gz_other, gz_other, send.at[18], recv.at[6], y_peer(d)).start()

    drain.append(lambda: pl.when(home != z)(gz_send.wait_send))
    drain.append(lambda: pl.when(home == z)(lambda: settle(gz.at[pl.ds(0, 112)], send.at[9])))
    drain.append(lambda: pl.when(home == z)(lambda: settle(gz.at[pl.ds(0, 112)], send.at[18])))
    z3_end(1)
    z3_end(2)
    z3_end(3)
    pl.when(home == z)(lambda: settle(gz.at[pl.ds(0, 112)], recv.at[6]))
    pl.when(home != z)(lambda: settle(gz, recv.at[6]))
    rows_z = parts(gz[...])

    def tile_of():
        return g_parts[0].reshape(256, 512), g_parts[1].reshape(256, 512)

    st[...] = by_rows(tile_of(), rows_z)
    for k in ALONG_X:
        remote(st, st_in.at[k - 1], send.at[14], recv.at[9], x_peer(k)).start()
    sent(st_in, send.at[14])

    @pl.when(x == zh)
    def _():
        cols = grad.at[:, :, :, pl.ds(pl.multiple_of(z % 4 * 128, 128), 128)]
        for k in ALONG_X:
            remote(cols, hl.at[0], send.at[13], recv.at[8], x_peer(k)).start()
        pltpu.make_async_copy(cols, hl.at[0], recv.at[8]).start()

    drain.append(lambda: pl.when(x == zh)(lambda: settle(st_in, send.at[13])))
    settle(hl.at[1], recv.at[4])
    settle(st_in, recv.at[9])
    st_sum[...] = st[...] + (st_in[0] + st_in[1] + st_in[2])
    lt = 0.9 * hl[1].reshape(256, 128) + 0.1 * st_sum[...]
    turned[...] = lt
    ur[0] = by_columns(lt, tile_of())

    def block_at(ref, d, *lead):
        r = pl.multiple_of((flip(c, d % 2) + 2 * flip(yl, d // 2 % 2)) * 32, 32)
        col = pl.multiple_of(flip(yh, d // 4) * 256, 256)
        return ref.at[(*lead, pl.ds(r, 32), pl.ds(col, 256))]

    for d in ALONG_Y:
        remote(
            block_at(ur, d, 0), ur_in.at[0, d - 1], send.at[15], recv.at[10], y_peer(d)
        ).start()
    sent(ur_in.at[0], send.at[15])
    own = turned[pl.ds(pl.multiple_of(x * 64, 64), 64), :]
    la[ylc] = own
    for d in range(1, 4):
        remote(la.at[ylc], la.at[ylc], send.at[16], recv.at[11], y_peer(d)).start()
    sent(qg_in, send.at[16])
    lane = lax.broadcasted_iota(jnp.int32, (1, 128), 1)

    def sum_in_plane(n, values):
        v = jnp.zeros((1, 128), F32)
        for i, value in enumerate(values):
            v = jnp.where(lane == i, value, v)
        s_own[n] = v

        for d in IN_PLANE:
            remote(s_own.at[n], s1_in.at[n, d - 1], s_sems.at[0, n], s_sems.at[1, n], plane_peer(d)).start()
        sent(s1_in.at[n], s_sems.at[0, n])

    def sum_along_z(n):
        settle(s1_in.at[n], s_sems.at[1, n])
        s1_sum[n] = s_own[n] + jnp.sum(s1_in[n], axis=0)

        for k in ALONG_Z:
            remote(s1_sum.at[n], s2_in.at[n, k - 1], s_sems.at[2, n], s_sems.at[3, n], z_peer(k)).start()
        sent(s2_in.at[n], s_sems.at[2, n])

    def sums(n, count):
        settle(s2_in.at[n], s_sems.at[3, n])
        v = s1_sum[n] + jnp.sum(s2_in[n], axis=0)
        picked = [jnp.where(lane == i, v, 0.0) for i in range(count)]
        return [jnp.sum(p, axis=1, keepdims=True) for p in picked]

    settle(hl.at[0], recv.at[8])
    ur[1] = by_columns(hl[0].reshape(256, 128), tile_of())
    for d in ALONG_Y:
        remote(
            block_at(ur, d, 1), ur_in.at[1, d - 1], send.at[0], recv.at[5], y_peer(d)
        ).start()
    drain.append(lambda: settle(ur_in.at[1], send.at[0]))
    sum_in_plane(0, (total(own), total(piece[...])))

    settle(ur_in.at[0], recv.at[10])
    u_block = block_at(ur, 0, 0)[...]
    for d in range(7):
        u_block = u_block + ur_in[0, d]
    ub[...] = u_block
    u_half[...] = u_block.astype(jnp.bfloat16)
    block_at(uz, 0)[...] = u_half[...]
    for d in ALONG_Y:
        remote(u_half, block_at(uz, 0), send.at[17], recv.at[12], y_peer(d)).start()
    sent(uz.at[pl.ds(0, 112)], send.at[17])
    sum_along_z(0)

    settle(uz.at[pl.ds(0, 112)], recv.at[12])
    rows_u = (uz[...],)
    su[...] = by_rows(tile_of(), rows_u).astype(jnp.bfloat16)
    for k in ALONG_X:
        remote(su, su_in.at[k - 1], send.at[22], recv.at[17], x_peer(k)).start()
    sent(su_in, send.at[22])
    settle(ur_in.at[1], recv.at[5])
    r_block = block_at(ur, 0, 1)[...]
    for d in range(7):
        r_block = r_block + ur_in[1, d]
    right = 0.9 * rs_ref[...] + 0.1 * r_block
    out_ref[1] = right
    sum_in_plane(1, (total(right),))
    pl.when(z1 == yh)(lambda: settle(stat.at[:, 0], recv.at[3]))
    pl.when(z1 != yh)(lambda: settle(stat, recv.at[3]))
    qg[...] = by_rows((stat[...].reshape(256, 512),), rows_z).reshape(4, 64, 128)
    for k in ALONG_X:
        to = lax.rem(x + k, 4)
        remote(qg.at[to], qg_in.at[k - 1], send.at[12], recv.at[7], x_peer(k)).start()
    sent(qg_in, send.at[12])
    qu[...] = by_rows((stat[...].reshape(256, 512),), rows_u).astype(jnp.bfloat16).reshape(4, 64, 128)
    for k in ALONG_X:
        to = lax.rem(x + k, 4)
        remote(qu.at[to], qu_in.at[k - 1], send.at[23], recv.at[18], x_peer(k)).start()
    sent(qu_in, send.at[23])
    sum_along_z(1)

    def assembled(slots):
        v = slots[...].reshape(4, 2, 32, 128)
        whole = jnp.concatenate([v[i, b] for b in range(2) for i in range(4)], axis=0)
        return whole.T

    settle(la.at[pl.ds(0, 3)], recv.at[11])
    lt_rows = assembled(la)
    uz_rows = pl.ds(pl.multiple_of(ylc * 32, 32), 32)
    pr[:, 0:256] = lt_rows
    out_ref[0] = pr[uz_rows, 0:256]

    settle(su_in, recv.at[17])
    s_u = su[...].astype(F32)
    for i in range(3):
        s_u = s_u + su_in[i].astype(F32)
    settle(qg_in, recv.at[7])
    settle(qu_in, recv.at[18])
    left_total, grad_total = sums(0, 2)
    left_scale = jnp.sqrt(left_total / B + 1e-06)
    q_g = qg[x] + qg_in[0] + qg_in[1] + qg_in[2]
    q_u = qu[x].astype(F32)
    for i in range(3):
        q_u = q_u + qu_in[i].astype(F32)
    q_sum[...] = 0.9 * (5.0 * q_g - q_u / left_scale)
    qa[ylc] = q_sum[...]
    for d in range(1, 4):
        remote(q_sum, qa.at[ylc], send.at[24], recv.at[19], y_peer(d)).start()
    sent(qg_in, send.at[24])
    pr[...] = by_columns(0.1 * (5.0 * st_sum[...] - s_u / left_scale), tile_of())
    for d in ALONG_Y:
        remote(block_at(pr, d), pr_in.at[d - 1], send.at[25], recv.at[20], y_peer(d)).start()
    sent(pr_in, send.at[25])
    pre_left = 5.0 * block_at(gz, 0)[...] - ub[...] / left_scale
    settle(qa.at[pl.ds(0, 3)], recv.at[19])
    turned[pl.ds(0, 128), :] = assembled(qa)[:, 0:128]
    turned[pl.ds(128, 128), :] = assembled(qa)[:, 128:256]
    low = turned[pl.ds(pl.multiple_of(ylc * 32, 32), 32), :]
    high = turned[pl.ds(pl.multiple_of(128 + ylc * 32, 32), 32), :]
    product = jnp.concatenate([low, high], axis=1) + block_at(pr, 0)[...]
    settle(pr_in, recv.at[20])
    for d in range(7):
        product = product + pr_in[d]
    (right_total,) = sums(1, 1)
    right_scale = jnp.sqrt(right_total / B + 1e-06)
    pre = 5.0 * pre_left - product / right_scale
    sum_in_plane(2, (total(pre),))
    sum_along_z(2)
    (pre_total,) = sums(2, 1)
    out_ref[2] = pre * (jnp.sqrt(grad_total + 1e-06) / jnp.sqrt(pre_total + 1e-06))

    for wait in drain:
        wait()


def local(activations, out_grads, left_stat, right_stat):
    vmem = pl.BlockSpec(memory_space=pltpu.VMEM)
    block = jax.ShapeDtypeStruct((32, 256), F32)
    bf16 = jnp.bfloat16
    shapes = [
        ((TOKENS, 256), bf16), ((TOKENS, 256), bf16),
        ((32, 256), F32), ((32, 256), F32),
        ((3, TOKENS, 256), bf16), ((TOKENS, 256), bf16),
        ((4, 2, 2, 2, 32, 512), F32), ((4, 2, 2, 32, 512), F32),
        ((4, 2, 2, 32, 512), F32), ((4, 2, 32, 512), F32),
        ((4, 2, 32, 512), F32), ((4, 3, 16, 512), F32),
        ((4, 16, 512), F32), ((4, 3, 16, 512), F32),
        ((4, 2, 32, 512), F32), ((2, 4, 64, 512), bf16), ((128, 512), F32),
        ((4, 2, 32, 512), bf16), ((32, 256), bf16),
        ((4, 2, 32, 128), F32), ((2, 4, 2, 32, 128), F32),
        ((256, 128), F32), ((3, 256, 128), F32), ((256, 128), F32),
        ((4, 64, 128), F32), ((3, 64, 128), F32),
        ((2, 128, 512), F32), ((2, 7, 32, 256), F32),
        ((4, 64, 128), F32), ((256, 128), F32), ((32, 256), F32), ((32, 256), bf16), ((128, 512), bf16),
        ((256, 128), bf16), ((3, 256, 128), bf16),
        ((4, 64, 128), bf16), ((3, 64, 128), bf16),
        ((128, 512), F32), ((7, 32, 256), F32),
        ((64, 128), F32), ((4, 64, 128), F32),
        ((3, 1, 128), F32), ((3, 31, 1, 128), F32),
        ((3, 1, 128), F32), ((3, 15, 1, 128), F32),
    ]
    dma = pltpu.SemaphoreType.DMA
    sems = [dma, dma((3, 2)), dma((26,)), dma((22,))] + [dma((4,))] * 12
    sems += [dma((4, 3)), pltpu.SemaphoreType.REGULAR((3,))]
    out = pl.pallas_call(
        kernel,
        out_shape=jax.ShapeDtypeStruct((3, 32, 256), F32),
        in_specs=[pl.BlockSpec(memory_space=pl.ANY)] * 4,
        out_specs=vmem,
        scratch_shapes=[pltpu.VMEM(s, d) for s, d in shapes] + sems,
        compiler_params=pltpu.CompilerParams(
            collective_id=0, has_side_effects=True, vmem_limit_bytes=60 * 2**20
        ),
        cost_estimate=pl.CostEstimate(flops=2 * 10**9, bytes_accessed=4 * 10**6, transcendentals=0),
    )(activations, out_grads, left_stat, right_stat)
    return out[0], out[1], out[2]


def solution(mesh):
    finer = Mesh(mesh.devices.reshape(16, 2, 2, 4, 2), ("z", "yl", "c", "x", "yh"))
    spec = P(DP, TENSOR)
    return jax.shard_map(
        local,
        mesh=finer,
        in_specs=(spec,) * 4,
        out_specs=(spec,) * 3,
        check_vma=False,
    )
```
